128 devices in a mesh: cls: 4 (over z_lo, core), dom: 32 (over x, z_hi, y).
Axes of the slice: x: 4, y: 4, z: 4 (z_hi: 2, z_lo: 2; z = z_hi * 2 + z_lo), core: 2. Of those that a mesh axis runs over, the one named last changes fastest.
Arguments:
- particles: bfloat16 [12288, 128, 128], P('dom'), may hold values from -600 to 600
- references: bfloat16 [128, 128, 128], P('cls', 'dom'), may hold values from -0.6 to 0.6
- ctf_table: float32 [64, 128], replicated, may hold values from 0.1 to 1
- noise_inv: float32 [128], replicated, may hold values from 0.05 to 0.5
- groups: int32 [12288], P('dom'), may hold values from 0 to 63
- prior_rot: int32 [12288], P('dom'), may hold values from 0 to 15
Outputs:
- new_refs: float32 [128, 128, 128], P('cls', 'dom')
- loglik: float32 [12288], P('dom')
The draws below stay inside these ranges and needn't reach their ends.
All inputs are finite; a program needn't handle non-finite values.
Results may differ from the reference program's by a relative error of at most 0.0026.
Values may be sent and summed in bfloat16 or wider, within the bound.
No kernel may reach another device: no remote copies, remote signals or barrier semaphores. Data moves between devices by JAX's collectives and lax.ppermute only.
A program may use at most 192 MiB of HBM per device.

```python
import math
import jax
import jax.numpy as jnp
from jax import lax

CLASSES = 128
CYCLES = 128
ANGLES = 128
ROTS = 16
GROUPS = 64
PARTICLES = 12288


def shared_refs(key):
    base = jax.random.normal(key, (CLASSES, CYCLES, ANGLES), jnp.float32) * 0.1
    return jnp.clip(base, -0.6, 0.6)


def draw_references(key, part):
    return shared_refs(key).astype(jnp.bfloat16)


def turned_refs(refs, picked, turned):
    aligned = refs[picked]
    angle_index = jnp.arange(ANGLES, dtype=jnp.int32)
    source = (angle_index[None, :] - turned[:, None] * (ANGLES // ROTS)) % ANGLES
    return jnp.take_along_axis(aligned, source[:, None, :], axis=2)


def draw_particles(key, part):
    refs = shared_refs(key).astype(jnp.bfloat16).astype(jnp.float32)
    key = jax.random.fold_in(key, 7)
    noise_key = jax.random.fold_in(key, 0)
    pick_key = jax.random.fold_in(key, 2)
    class_key = jax.random.fold_in(key, 3)
    turn_key = jax.random.fold_in(key, 4)
    power_key = jax.random.fold_in(key, 5)
    other_key = jax.random.fold_in(key, 6)
    other_turn = jax.random.fold_in(key, 7)
    noise = jnp.clip(jax.random.normal(noise_key, (PARTICLES, CYCLES, ANGLES), jnp.float32), -6.0, 6.0)
    start = jax.random.randint(pick_key, (), 0, 32)
    index = jnp.arange(PARTICLES, dtype=jnp.int32)
    chosen = (index + start) % 32 == 0
    picked = jax.random.randint(class_key, (PARTICLES,), 0, CLASSES)
    second = (picked + jax.random.randint(other_key, (PARTICLES,), 1, CLASSES)) % CLASSES
    turned = jax.random.randint(turn_key, (PARTICLES,), 0, ROTS)
    turned_b = jax.random.randint(other_turn, (PARTICLES,), 0, ROTS)
    strength = jnp.exp(jax.random.uniform(power_key, (PARTICLES,), jnp.float32, 5.4, 6.1))
    strength = strength * (1024.0 / (CYCLES * ANGLES))
    first_img = turned_refs(refs, picked, turned)
    second_img = turned_refs(refs, second, turned_b)
    boost = jnp.where(chosen, strength, 0.0)[:, None, None]
    values = noise + boost * (first_img + 0.97 * second_img)
    return values.astype(jnp.bfloat16)


def touch_ends(result, key, low, top_value):
    index_at = [jax.random.randint(jax.random.fold_in(key, axis), (), 0, length) for axis, length in enumerate(result.shape)]
    longest = result.shape.index(max(result.shape))
    beside = index_at[:longest] + [(index_at[longest] + 1) % result.shape[longest]] + index_at[longest + 1:]
    return result.at[tuple(index_at)].set(low).at[tuple(beside)].set(top_value)


def setup_inputs(seed: int = 0) -> dict:
    seeds = jax.random.split(jax.random.key(seed), 7)
    particles = draw_particles(jax.random.fold_in(seeds[6], 71), 0)
    references = draw_references(jax.random.fold_in(seeds[6], 71), 0)
    ctf_table = jnp.clip(jax.random.uniform(seeds[2], (GROUPS, CYCLES), jnp.float32, 0.1, 1.0), 0.1, 1.0)
    noise_inv = jnp.clip(jnp.exp(jax.random.uniform(seeds[3], (CYCLES,), jnp.float32, math.log(0.05), math.log(0.5))), 0.05, 0.5)
    groups = touch_ends(jax.random.randint(seeds[4], (PARTICLES,), 0, GROUPS), jax.random.fold_in(seeds[4], 1), 0, GROUPS - 1).astype(jnp.int32)
    prior_rot = touch_ends(jax.random.randint(seeds[5], (PARTICLES,), 0, ROTS), jax.random.fold_in(seeds[5], 1), 0, ROTS - 1).astype(jnp.int32)
    return {"particles": particles, "references": references, "ctf_table": ctf_table, "noise_inv": noise_inv, "groups": groups, "prior_rot": prior_rot}


PRIOR_WEIGHT = 0.02
TIKHONOV = 1.0


def reference(particles, references, ctf_table, noise_inv, groups, prior_rot):
    step = ANGLES // ROTS
    cycle_weight = ctf_table[groups] * noise_inv[None, :]
    weighted = (particles.astype(jnp.float32) * cycle_weight[:, :, None]).astype(jnp.bfloat16)
    flat = weighted.reshape(PARTICLES, CYCLES * ANGLES)
    rotated = jnp.stack([jnp.roll(references, turn * step, axis=2) for turn in range(ROTS)])
    rotated = rotated.reshape(ROTS * CLASSES, CYCLES * ANGLES)
    corr = lax.dot_general(flat, rotated, (((1,), (1,)), ((), ())), preferred_element_type=jnp.float32)
    corr = corr.reshape(PARTICLES, ROTS, CLASSES)
    ctf_power = ctf_table * ctf_table * noise_inv[None, :]
    ref_float = references.astype(jnp.float32)
    cycle_power = jnp.sum(ref_float * ref_float, axis=2)
    norm_table = jnp.dot(ctf_power, cycle_power.T, precision=lax.Precision.HIGHEST)
    norm_part = norm_table[groups]
    turns = jnp.arange(ROTS, dtype=jnp.int32)
    offset = (turns[None, :] - prior_rot[:, None]) % ROTS
    distance = jnp.minimum(offset, ROTS - offset).astype(jnp.float32)
    prior = -PRIOR_WEIGHT * distance * distance
    score = corr - 0.5 * norm_part[:, None, :] + prior[:, :, None]
    peak = jnp.max(score, axis=(1, 2))
    expo = jnp.exp(score - peak[:, None, None])
    total = jnp.sum(expo, axis=(1, 2))
    loglik = peak + jnp.log(total)
    resp = (expo / total[:, None, None]).astype(jnp.bfloat16)
    sums = lax.dot_general(resp.reshape(PARTICLES, ROTS * CLASSES), flat, (((0,), (0,)), ((), ())), preferred_element_type=jnp.float32)
    sums = sums.reshape(ROTS, CLASSES, CYCLES, ANGLES)
    numer = jnp.zeros((CLASSES, CYCLES, ANGLES), jnp.float32)
    for turn in range(ROTS):
        numer = numer + jnp.roll(sums[turn], -turn * step, axis=2)
    class_weight = jnp.sum(resp.astype(jnp.float32), axis=1)
    denom = jnp.dot(class_weight.T, ctf_power[groups], precision=lax.Precision.HIGHEST)
    new_refs = numer / (denom[:, :, None] + TIKHONOV)
    return new_refs, loglik
```

```python
import jax
import jax.numpy as jnp
from jax import lax
from jax.experimental import pallas as pl
from jax.experimental.pallas import tpu as pltpu
from jax.sharding import PartitionSpec as P

ROTS = 16
PRIOR_WEIGHT = 0.02
TIKHONOV = 1.0
F32 = jnp.float32
BF16 = jnp.bfloat16
NX, NZ, NY = 4, 2, 4
VMEM = pl.BlockSpec(memory_space=pltpu.VMEM)
MIB = 2**20


def params(mib):
    return pltpu.CompilerParams(vmem_limit_bytes=mib * MIB)


def cost(flops, nbytes):
    return pl.CostEstimate(flops=flops, bytes_accessed=nbytes, transcendentals=0)


def coords(i):
    return i // (NZ * NY), (i // NY) % NZ, i % NY


def shift(dx, dz, dy):
    pairs = []
    for i in range(NX * NZ * NY):
        x, z, y = coords(i)
        pairs.append((i, ((x + dx) % NX) * NZ * NY + ((z + dz) % NZ) * NY + (y + dy) % NY))
    return pairs


def send(value, dx, dz, dy):
    return lax.ppermute(value, "dom", shift(dx, dz, dy))


def split2(value):
    high = value.astype(BF16)
    low = (value - high.astype(F32)).astype(BF16)
    return high, low


def setup_kernel(groups_ref, ctf_ref, noise_ref, weight_ref, power_ref):
    group_count, cycles = ctf_ref.shape
    count = groups_ref.shape[1]
    choose = (
        lax.broadcasted_iota(jnp.int32, (group_count, count), 0) == groups_ref[...]
    ).astype(F32)
    pick = lambda table: lax.dot_general(
        choose, table, (((0,), (0,)), ((), ())), precision=lax.Precision.HIGHEST,
        preferred_element_type=F32,
    )
    ctf = ctf_ref[...]
    noise = noise_ref[...]
    weight_ref[...] = pick(ctf) * noise
    high, low = split2(pick(ctf * ctf * noise))
    power_ref[:, :cycles] = high
    power_ref[:, cycles:] = low


def setup(groups, ctf_table, noise_inv):
    count = groups.shape[0]
    cycles = ctf_table.shape[1]
    return pl.pallas_call(
        setup_kernel,
        out_shape=(
            jax.ShapeDtypeStruct((count, cycles), F32),
            jax.ShapeDtypeStruct((count, 2 * cycles), BF16),
        ),
        in_specs=[VMEM] * 3,
        out_specs=(VMEM, VMEM),
        compiler_params=params(16),
        name="setup",
    )(groups.reshape(1, count), ctf_table, noise_inv.reshape(1, cycles))


def weigh_kernel(particles_ref, weight_ref, out_ref, wide):
    rows, cycles, _ = particles_ref.shape
    pitch = cycles + 1
    start = pl.multiple_of(pl.program_id(0) * rows, 16)
    weight = weight_ref[...]
    for n in range(rows):
        wide[pl.ds(n * pitch, cycles), :] = particles_ref[n].astype(F32)
    for q in range(cycles):
        image = wide[pl.ds(q, rows, stride=pitch), :]
        out_ref[q, pl.ds(start, rows), :] = (image * weight[:, q : q + 1]).astype(BF16)


def weigh(particles, weight, part, parts):
    count, cycles, angles = particles.shape
    here = count // parts
    rows = 48
    steps = here // rows
    return pl.pallas_call(
        weigh_kernel,
        out_shape=pltpu.VMEM((cycles, here, angles), BF16),
        grid=(steps,),
        in_specs=[
            pl.BlockSpec((rows, cycles, angles), lambda i: (part * steps + i, 0, 0)),
            pl.BlockSpec((rows, cycles), lambda i: (part * steps + i, 0)),
        ],
        out_specs=VMEM,
        scratch_shapes=[pltpu.VMEM((rows * (cycles + 1) + 8, angles), F32)],
        compiler_params=params(16),
        cost_estimate=cost(0, here * cycles * angles * 16),
        name="weigh",
    )(particles, weight)


def cycle_of(dx, j):
    dom = lax.axis_index("dom")
    x, z, y = dom // (NZ * NY), (dom // NY) % NZ, dom % NY
    dy, dz, i = j // (4 * NZ), (j // 4) % NZ, j % 4
    return ((x + dx) % NX) * (4 * NZ * NY) + ((z + dz) % NZ) * (4 * NY) + ((y + dy) % NY) * 4 + i


def correlate_steps(shifts, block_refs, image_refs, turned, total, power):
    classes, angles = block_refs[0].shape[1:]
    lane = lax.broadcasted_iota(jnp.int32, power.shape, 1)
    slot = 0
    for dx, block_ref in zip(shifts, block_refs):
        for j in range(0, block_ref.shape[0], 2):
            sides = []
            for i in range(2):
                piece = block_ref[j + i]
                cycle = cycle_of(dx, j + i)
                for turn in range(ROTS):
                    turned[slot % 4, turn * classes : (turn + 1) * classes, i * angles : (i + 1) * angles] = (
                        pltpu.roll(piece, 8 * turn, 1) if turn else piece
                    )
                wide = piece.astype(F32)
                power = jnp.where(lane == cycle, jnp.sum(wide * wide, axis=1, keepdims=True), power)
                sides.append(jnp.concatenate([ref[cycle] for ref in image_refs], axis=0))
            part = lax.dot_general(
                jnp.concatenate(sides, axis=1), turned[slot % 4], (((1,), (1,)), ((), ())),
                preferred_element_type=F32,
            )
            total = part if total is None else total + part
            slot += 1
    return total, power


def correlate(shifts, blocks, images, before):
    cycles = images[0].shape[0]
    angles = images[0].shape[2]
    count = sum(image.shape[1] for image in images)
    classes = blocks[0].shape[1]
    wide = ROTS * classes
    nb, ni = len(blocks), len(images)

    def kernel(*refs):
        block_refs, image_refs = refs[:nb], refs[nb : nb + ni]
        rest = refs[nb + ni :]
        if before is not None:
            total, power = rest[0][...], rest[1][...]
            rest = rest[2:]
        else:
            total, power = None, jnp.zeros((classes, cycles), F32)
        total_ref, power_ref, turned = rest
        total, power = correlate_steps(shifts, block_refs, image_refs, turned, total, power)
        total_ref[...] = total
        power_ref[...] = power

    extra = [] if before is None else list(before)
    return pl.pallas_call(
        kernel,
        out_shape=(pltpu.VMEM((count, wide), F32), pltpu.VMEM((classes, cycles), F32)),
        in_specs=[VMEM] * (nb + ni + len(extra)),
        out_specs=(VMEM, VMEM),
        scratch_shapes=[pltpu.VMEM((4, wide, 2 * angles), BF16)],
        compiler_params=params(24),
        cost_estimate=cost(2 * count * wide * 32 * nb * angles, 0),
        name="correlate",
    )(*blocks, *images, *extra)


def score(shifts, blocks, images, before, power_pair, prior_rot):
    cycles = images[0].shape[0]
    angles = images[0].shape[2]
    count = sum(image.shape[1] for image in images)
    classes = blocks[0].shape[1]
    wide = ROTS * classes
    nb, ni = len(blocks), len(images)

    def kernel(*refs):
        block_refs, image_refs = refs[:nb], refs[nb : nb + ni]
        total_ref, cycle_ref, pair_ref, prior_ref, expo_ref, stats_ref, turned = refs[nb + ni :]
        total, power = correlate_steps(
            shifts, block_refs, image_refs, turned, total_ref[...], cycle_ref[...]
        )
        high, low = split2(-0.5 * power)
        both = jnp.concatenate([high, high], axis=1)
        low_both = jnp.concatenate([low, low], axis=1)
        pair = pair_ref[...]
        norm = lax.dot_general(pair, both, (((1,), (1,)), ((), ())), preferred_element_type=F32)
        norm = norm + lax.dot_general(
            pair, low_both, (((1,), (1,)), ((), ())), preferred_element_type=F32
        )
        total = total + jnp.concatenate([norm] * ROTS, axis=1)
        hot = (
            lax.broadcasted_iota(jnp.int32, (2 * ROTS, count), 0) % ROTS == prior_ref[...]
        ).astype(BF16)
        row = lax.broadcasted_iota(jnp.int32, (2 * ROTS, wide), 0)
        turn = lax.broadcasted_iota(jnp.int32, (2 * ROTS, wide), 1) // classes
        offset = (turn - row + 2 * ROTS) % ROTS
        distance = jnp.minimum(offset, ROTS - offset).astype(F32)
        prior = -PRIOR_WEIGHT * distance * distance
        high, low = split2(prior)
        table = jnp.where(row < ROTS, high.astype(F32), low.astype(F32)).astype(BF16)
        total = total + lax.dot_general(
            hot, table, (((0,), (0,)), ((), ())), preferred_element_type=F32
        )
        peak = jnp.max(total, axis=1, keepdims=True)
        expo = jnp.exp(total - peak)
        expo_ref[...] = expo
        mass = jnp.sum(expo, axis=1, keepdims=True)
        lane = lax.broadcasted_iota(jnp.int32, (count, 128), 1)
        stats = jnp.transpose(jnp.where(lane < 64, peak, mass))
        stats_ref[0:8] = stats[0:8]
        stats_ref[8:16] = stats[64:72]

    return pl.pallas_call(
        kernel,
        out_shape=(pltpu.VMEM((count, wide), F32), jax.ShapeDtypeStruct((16, count), F32)),
        in_specs=[VMEM] * (nb + ni + 4),
        out_specs=(VMEM, VMEM),
        scratch_shapes=[pltpu.VMEM((4, wide, 2 * angles), BF16)],
        compiler_params=params(24),
        cost_estimate=cost(2 * count * wide * 32 * nb * angles, 0),
        name="score",
    )(*blocks, *images, *before, power_pair, prior_rot.reshape(1, count))


def turn_over_kernel(expo_ref, out_ref):
    out_ref[...] = jnp.transpose(expo_ref[...])


def turn_over(expo):
    count, wide = expo.shape
    return pl.pallas_call(
        turn_over_kernel,
        out_shape=pltpu.VMEM((wide, count), F32),
        in_specs=[VMEM],
        out_specs=VMEM,
        compiler_params=params(16),
        cost_estimate=cost(0, 4 * count * wide),
        name="turn_over",
    )(expo)


def share_kernel(expo_ref, own_ref, a_ref, b_ref, c_ref, pair_ref, resp_ref, loglik_ref, denom_ref):
    refs = (own_ref, a_ref, b_ref, c_ref)
    peaks = [ref[0:8] for ref in refs]
    peak = jnp.maximum(jnp.maximum(peaks[0], peaks[1]), jnp.maximum(peaks[2], peaks[3]))
    scales = [jnp.exp(value - peak) for value in peaks]
    total = sum(scale * ref[8:16] for scale, ref in zip(scales, refs))
    loglik_ref[...] = peak + jnp.log(total)
    factor = (scales[0] / total)[0:1]
    resp = (expo_ref[...] * factor).astype(BF16)
    resp_ref[...] = resp
    classes, cycles = denom_ref.shape
    rows = jnp.dot(resp, pair_ref[...], preferred_element_type=F32)
    rows = rows[:, :cycles] + rows[:, cycles:]
    denom = rows[:classes]
    for turn in range(1, ROTS):
        denom = denom + rows[turn * classes : (turn + 1) * classes]
    denom_ref[...] = denom


def share(expo, own, others, power_pair, classes):
    wide, count = expo.shape
    cycles = power_pair.shape[1] // 2
    return pl.pallas_call(
        share_kernel,
        out_shape=(
            pltpu.VMEM((wide, count), BF16),
            jax.ShapeDtypeStruct((8, count), F32),
            pltpu.VMEM((classes, cycles), F32),
        ),
        in_specs=[VMEM] * 6,
        out_specs=(VMEM, VMEM, VMEM),
        compiler_params=params(24),
        name="share",
    )(expo, own, *others, power_pair)


def pack_denom(denom):
    lane = lax.broadcasted_iota(jnp.int32, denom.shape, 1)
    high, low = split2(denom)
    packed = jnp.where(lane < 32, high.astype(F32), pltpu.roll(low.astype(F32), 32, 1))
    return jnp.where(lane < 64, packed, 0.0)


def join_denom(packed):
    lane = lax.broadcasted_iota(jnp.int32, packed.shape, 1)
    return jnp.where(lane < 32, packed + pltpu.roll(packed, 96, 1), 0.0)


def gather_sums(dx, resp, images, denom, dtype):
    classes, cycles = denom.shape
    angles = images[0].shape[2]
    wide, count = resp.shape
    length = 4 * NZ * NY
    ni = len(images)

    def kernel(*refs):
        resp_ref, image_refs = refs[0], refs[1 : 1 + ni]
        denom_ref, out_ref = refs[1 + ni :]
        for j in range(0, length, 2):
            side = jnp.concatenate(
                [
                    jnp.concatenate([ref[cycle_of(dx, j + i)] for ref in image_refs], axis=0)
                    for i in range(2)
                ],
                axis=1,
            )
            sums = jnp.dot(resp_ref[...], side, preferred_element_type=F32)
            for i in range(2):
                total = None
                for turn in range(ROTS):
                    piece = sums[turn * classes : (turn + 1) * classes, i * angles : (i + 1) * angles]
                    if turn:
                        piece = pltpu.roll(piece, angles - 8 * turn, 1)
                    total = piece if total is None else total + piece
                out_ref[j + i] = total.astype(dtype)
        x = lax.axis_index("dom") // (NZ * NY)
        offset = ((x + dx) % NX) * length
        mine = pltpu.roll(denom_ref[...], (cycles - offset) % cycles, 1)
        lane = lax.broadcasted_iota(jnp.int32, mine.shape, 1)
        if dtype == BF16:
            out_ref[length] = pack_denom(mine).astype(BF16)
        else:
            out_ref[length] = jnp.where(lane < length, mine, 0.0)

    return pl.pallas_call(
        kernel,
        out_shape=jax.ShapeDtypeStruct((length + 1, classes, angles), dtype),
        in_specs=[VMEM] * (ni + 2),
        out_specs=VMEM,
        compiler_params=params(24),
        cost_estimate=cost(2 * count * wide * length * angles, 0),
        name="gather_sums",
    )(resp, *images, denom)


def add_parts(own, others, ways):
    rows, classes, angles = own.shape
    length = (rows - 1) // ways

    def kernel(own_ref, *refs):
        others_ref, outs = refs[: len(others)], refs[len(others) :]
        total = own_ref[rows - 1]
        for ref in others_ref:
            total = total + ref[rows - 1].astype(F32)
        denom = join_denom(total)
        packed = pack_denom(denom).astype(BF16)
        for way in range(ways):
            for j in range(length):
                total = own_ref[way * length + j]
                for ref in others_ref:
                    total = total + ref[way * length + j].astype(F32)
                outs[way][j] = total.astype(outs[way].dtype)
            outs[way][length] = packed if way else denom

    shape = (length + 1, classes, angles)
    return pl.pallas_call(
        kernel,
        out_shape=tuple(
            jax.ShapeDtypeStruct(shape, BF16 if way else F32) for way in range(ways)
        ),
        in_specs=[VMEM] * (1 + len(others)),
        out_specs=(VMEM,) * ways,
        compiler_params=params(16),
        name="add_parts",
    )(own, *others)


def finish(own, other):
    rows, classes, angles = own.shape

    def kernel(own_ref, other_ref, out_ref):
        dom = lax.axis_index("dom")
        offset = ((dom // NY) % NZ) * (4 * NY) + (dom % NY) * 4
        denom = join_denom(own_ref[rows - 1] + other_ref[rows - 1].astype(F32))
        denom = pltpu.roll(denom, (angles - offset) % angles, 1) + TIKHONOV
        for i in range(rows - 1):
            numer = own_ref[i] + other_ref[i].astype(F32)
            out_ref[:, i, :] = numer / denom[:, i : i + 1]

    return pl.pallas_call(
        kernel,
        out_shape=jax.ShapeDtypeStruct((classes, rows - 1, angles), F32),
        in_specs=[VMEM, VMEM],
        out_specs=VMEM,
        compiler_params=params(16),
        name="finish",
    )(own, other)


def local(particles, references, ctf_table, noise_inv, groups, prior_rot):
    classes = references.shape[0]
    piece = jnp.transpose(references, (1, 0, 2))
    piece = jnp.concatenate([piece, send(piece, 0, 1, 0)], axis=0)
    piece = jnp.concatenate([piece] + [send(piece, 0, 0, -d) for d in (1, 2, 3)], axis=0)
    blocks = [piece] + [send(piece, -d, 0, 0) for d in (1, 2, 3)]

    weight, power_pair = setup(groups, ctf_table, noise_inv)
    parts = 4
    images = [weigh(particles, weight, part, parts) for part in range(parts)]

    before = correlate((0,), blocks[:1], images, None)
    before = correlate((1, 3), [blocks[1], blocks[3]], images, before)
    expo, stats = score((2,), [blocks[2]], images, before, power_pair, prior_rot)
    others = [lax.ppermute(stats, "cls", [(i, i ^ j) for i in range(4)]) for j in (1, 2, 3)]
    turned = turn_over(expo)
    resp, loglik, denom = share(turned, stats, others, power_pair, classes)

    arrived = []
    for d in (2, 1, 3):
        arrived.append(send(gather_sums(d, resp, images, denom, BF16), d, 0, 0))
    own = gather_sums(0, resp, images, denom, F32)
    pieces = add_parts(own, arrived, NY)
    arrived = [send(pieces[d], 0, 0, d) for d in (1, 2, 3)]
    pieces = add_parts(pieces[0], arrived, NZ)
    new_refs = finish(pieces[0], send(pieces[1], 0, 1, 0))
    return (new_refs, loglik[0])


def solution(mesh):
    in_specs = (P("dom", None, None), P("cls", "dom", None), P(), P(), P("dom"), P("dom"))
    out_specs = (P("cls", "dom", None), P("dom"))
    return jax.shard_map(local, mesh=mesh, in_specs=in_specs, out_specs=out_specs, check_vma=False)
```

```python
import jax
import jax.numpy as jnp
from jax import lax
from jax.experimental import pallas as pl
from jax.experimental.pallas import tpu as pltpu
from jax.sharding import PartitionSpec as P

ROTS = 16
PRIOR_WEIGHT = 0.02
TIKHONOV = 1.0
F32 = jnp.float32
BF16 = jnp.bfloat16
NX, NZ, NY = 4, 2, 4
VMEM = pl.BlockSpec(memory_space=pltpu.VMEM)
HBM = pl.BlockSpec(memory_space=pltpu.HBM)
MIB = 2**20
STREAMS = 1


def params(mib):
    return pltpu.CompilerParams(vmem_limit_bytes=mib * MIB)


def cost(flops, nbytes):
    return pl.CostEstimate(flops=flops // 64, bytes_accessed=nbytes // 64, transcendentals=0)


def coords(i):
    return i // (NZ * NY), (i // NY) % NZ, i % NY


def shift(dx, dz, dy):
    pairs = []
    for i in range(NX * NZ * NY):
        x, z, y = coords(i)
        pairs.append((i, ((x + dx) % NX) * NZ * NY + ((z + dz) % NZ) * NY + (y + dy) % NY))
    return pairs


def send(value, dx, dz, dy):
    return lax.ppermute(value, "dom", shift(dx, dz, dy))


def split2(value):
    high = value.astype(BF16)
    low = (value - high.astype(F32)).astype(BF16)
    return high, low


def load_rows(source, start, target, sems, first):
    rows = target.shape[0] // STREAMS
    return [
        pltpu.make_async_copy(
            source.at[pl.ds(start + i * rows, rows)], target.at[pl.ds(i * rows, rows)], sems.at[first + i]
        )
        for i in range(STREAMS)
    ]


def setup_kernel(groups_ref, ctf_hbm, noise_hbm, particles_hbm, weight_ref, power_ref, first_ref, ctf_ref, noise_ref, sems):
    count = groups_ref.shape[0]
    group_count, cycles = ctf_ref.shape
    copies = [
        pltpu.make_async_copy(ctf_hbm, ctf_ref, sems.at[0]),
        pltpu.make_async_copy(noise_hbm, noise_ref, sems.at[1]),
    ]
    copies += load_rows(particles_hbm, 0, first_ref, sems, 2)
    for copy in copies:
        copy.start()
    choose = (
        lax.broadcasted_iota(jnp.int32, (group_count, count), 0) == groups_ref[...].reshape(1, count)
    ).astype(F32)
    pick = lambda table: lax.dot_general(
        choose, table, (((0,), (0,)), ((), ())), precision=lax.Precision.HIGHEST,
        preferred_element_type=F32,
    )
    copies[0].wait()
    copies[1].wait()
    ctf = ctf_ref[...]
    noise = noise_ref[...]
    weight_ref[...] = pick(ctf) * noise
    high, low = split2(pick(ctf * ctf * noise))
    power_ref[:, :cycles] = high
    power_ref[:, cycles:] = low
    for copy in copies[2:]:
        copy.wait()


def setup(groups, ctf_table, noise_inv, particles, parts):
    count = groups.shape[0]
    cycles = ctf_table.shape[1]
    return pl.pallas_call(
        setup_kernel,
        out_shape=(
            jax.ShapeDtypeStruct((count, cycles), F32),
            jax.ShapeDtypeStruct((count, 2 * cycles), BF16),
            pltpu.VMEM((count // parts,) + particles.shape[1:], BF16),
        ),
        in_specs=[VMEM, HBM, HBM, HBM],
        out_specs=(VMEM, VMEM, VMEM),
        scratch_shapes=[
            pltpu.VMEM(ctf_table.shape, F32),
            pltpu.VMEM((1, cycles), F32),
            pltpu.SemaphoreType.DMA((2 + STREAMS,)),
        ],
        compiler_params=params(16),
        name="setup",
    )(groups, ctf_table, noise_inv, particles)


def weigh(particles, here, weight, part, parts):
    count, cycles, angles = particles.shape
    rows = count // parts
    pitch = cycles + 1
    last = part == parts - 1

    def kernel(particles_hbm, here_ref, weight_ref, out_ref, token_ref, *refs):
        if not last:
            next_ref, wide, sems = refs
            copies = load_rows(particles_hbm, (part + 1) * rows, next_ref, sems, 0)
            for copy in copies:
                copy.start()
        else:
            wide = refs[0]
        values = weight_ref[part * rows : (part + 1) * rows]
        token_ref[...] = values[0:8]
        for n in range(rows):
            wide[pl.ds(n * pitch, cycles), :] = here_ref[n].astype(F32)
        pair = jnp.concatenate(split2(values), axis=1)
        row = lax.broadcasted_iota(jnp.int32, (16, 2 * angles), 0)
        side = lax.broadcasted_iota(jnp.int32, (16, 2 * angles), 1) // angles
        for q in range(0, cycles, 2):
            if q % 6 < 4:
                base = q // 16 * 16
                pick = [jnp.where(row - side == q % 16, 1.0, 0.0).astype(BF16)]
                if base:
                    pick = [jnp.zeros((base, 2 * angles), BF16)] + pick
                if base + 16 < cycles:
                    pick = pick + [jnp.zeros((cycles - 16 - base, 2 * angles), BF16)]
                spread = jnp.dot(
                    pair, jnp.concatenate(pick * 2, axis=0), preferred_element_type=F32
                )
                scales = [spread[:, :angles], spread[:, angles:]]
            else:
                scales = [values[:, q : q + 1], values[:, q + 1 : q + 2]]
            for i in range(2):
                image = wide[pl.ds(q + i, rows, stride=pitch), :]
                out_ref[q + i] = (image * scales[i]).astype(BF16)
        if not last:
            for copy in copies:
                copy.wait()

    shape = (rows, cycles, angles)
    return pl.pallas_call(
        kernel,
        out_shape=(pltpu.VMEM((cycles, rows, angles), BF16), jax.ShapeDtypeStruct((8, cycles), F32))
        + (() if last else (pltpu.VMEM(shape, BF16),)),
        in_specs=[HBM, VMEM, VMEM],
        out_specs=(VMEM,) * (2 if last else 3),
        scratch_shapes=[pltpu.VMEM((rows * pitch + 8, angles), F32)]
        + ([] if last else [pltpu.SemaphoreType.DMA((STREAMS,))]),
        compiler_params=params(16),
        cost_estimate=cost(0, rows * cycles * angles * 16),
        name="weigh",
    )(particles, here, weight)


def join(pieces, *tokens, turned=False):
    rows, classes, angles = pieces[0].shape
    if turned:
        rows, classes = classes, rows

    def kernel(*refs):
        out_ref = refs[-1]
        for i, ref in enumerate(refs[: len(pieces)]):
            for j in range(rows):
                out_ref[i * rows + j] = ref[:, j, :] if turned else ref[j]

    return pl.pallas_call(
        kernel,
        out_shape=jax.ShapeDtypeStruct((rows * len(pieces), classes, angles), BF16),
        in_specs=[VMEM] * len(pieces) + [pl.BlockSpec(memory_space=pl.ANY)] * len(tokens),
        out_specs=VMEM,
        compiler_params=params(16),
        name="join",
    )(*pieces, *tokens)


def cycle_of(dx, j):
    dom = lax.axis_index("dom")
    x, z, y = dom // (NZ * NY), (dom // NY) % NZ, dom % NY
    dy, dz, i = j // (4 * NZ), (j // 4) % NZ, j % 4
    return ((x + dx) % NX) * (4 * NZ * NY) + ((z + dz) % NZ) * (4 * NY) + ((y + dy) % NY) * 4 + i


def correlate_steps(shifts, block_refs, image_refs, turned, total, power):
    classes, angles = block_refs[0].shape[1:]
    lane = lax.broadcasted_iota(jnp.int32, power.shape, 1)
    slot = 0
    for dx, block_ref in zip(shifts, block_refs):
        for j in range(0, block_ref.shape[0], 2):
            sides = []
            for i in range(2):
                piece = block_ref[j + i]
                cycle = cycle_of(dx, j + i)
                for turn in range(ROTS):
                    turned[slot % 4, turn * classes : (turn + 1) * classes, i * angles : (i + 1) * angles] = (
                        pltpu.roll(piece, 8 * turn, 1) if turn else piece
                    )
                wide = piece.astype(F32)
                power = jnp.where(lane == cycle, jnp.sum(wide * wide, axis=1, keepdims=True), power)
                sides.append(jnp.concatenate([ref[cycle] for ref in image_refs], axis=0))
            part = lax.dot_general(
                jnp.concatenate(sides, axis=1), turned[slot % 4], (((1,), (1,)), ((), ())),
                preferred_element_type=F32,
            )
            total = part if total is None else total + part
            slot += 1
    return total, power


def correlate(shifts, blocks, images, before):
    cycles = images[0].shape[0]
    angles = images[0].shape[2]
    count = sum(image.shape[1] for image in images)
    classes = blocks[0].shape[1]
    wide = ROTS * classes
    nb, ni = len(blocks), len(images)

    def kernel(*refs):
        block_refs, image_refs = refs[:nb], refs[nb : nb + ni]
        rest = refs[nb + ni :]
        if before is not None:
            total, power = rest[0][...], rest[1][...]
            rest = rest[2:]
        else:
            total, power = None, jnp.zeros((classes, cycles), F32)
        total_ref, power_ref, turned = rest
        total, power = correlate_steps(shifts, block_refs, image_refs, turned, total, power)
        total_ref[...] = total
        power_ref[...] = power

    extra = [] if before is None else list(before)
    return pl.pallas_call(
        kernel,
        out_shape=(pltpu.VMEM((count, wide), F32), pltpu.VMEM((classes, cycles), F32)),
        in_specs=[VMEM] * (nb + ni + len(extra)),
        out_specs=(VMEM, VMEM),
        scratch_shapes=[pltpu.VMEM((4, wide, 2 * angles), BF16)],
        compiler_params=params(24),
        cost_estimate=cost(2 * count * wide * 32 * nb * angles, 0),
        name="correlate",
    )(*blocks, *images, *extra)


def score(shifts, blocks, images, before, power_pair, prior_rot):
    cycles = images[0].shape[0]
    angles = images[0].shape[2]
    count = sum(image.shape[1] for image in images)
    classes = blocks[0].shape[1]
    wide = ROTS * classes
    nb, ni = len(blocks), len(images)

    def kernel(*refs):
        block_refs, image_refs = refs[:nb], refs[nb : nb + ni]
        total_ref, cycle_ref, pair_ref, prior_ref, expo_ref, stats_ref, turned = refs[nb + ni :]
        total, power = correlate_steps(
            shifts, block_refs, image_refs, turned, total_ref[...], cycle_ref[...]
        )
        high, low = split2(-0.5 * power)
        both = jnp.concatenate([high, high], axis=1)
        low_both = jnp.concatenate([low, low], axis=1)
        pair = pair_ref[...]
        norm = lax.dot_general(pair, both, (((1,), (1,)), ((), ())), preferred_element_type=F32)
        norm = norm + lax.dot_general(
            pair, low_both, (((1,), (1,)), ((), ())), preferred_element_type=F32
        )
        total = total + jnp.concatenate([norm] * ROTS, axis=1)
        hot = (
            lax.broadcasted_iota(jnp.int32, (2 * ROTS, count), 0) % ROTS == prior_ref[...]
        ).astype(BF16)
        row = lax.broadcasted_iota(jnp.int32, (2 * ROTS, wide), 0)
        turn = lax.broadcasted_iota(jnp.int32, (2 * ROTS, wide), 1) // classes
        offset = (turn - row + 2 * ROTS) % ROTS
        distance = jnp.minimum(offset, ROTS - offset).astype(F32)
        prior = -PRIOR_WEIGHT * distance * distance
        high, low = split2(prior)
        table = jnp.where(row < ROTS, high.astype(F32), low.astype(F32)).astype(BF16)
        total = total + lax.dot_general(
            hot, table, (((0,), (0,)), ((), ())), preferred_element_type=F32
        )
        peak = jnp.max(total, axis=1, keepdims=True)
        expo = jnp.exp(total - peak)
        expo_ref[...] = expo
        mass = jnp.sum(expo, axis=1, keepdims=True)
        lane = lax.broadcasted_iota(jnp.int32, (count, 128), 1)
        stats = jnp.transpose(jnp.where(lane < 64, peak, mass))
        stats_ref[0:8] = stats[0:8]
        stats_ref[8:16] = stats[64:72]

    return pl.pallas_call(
        kernel,
        out_shape=(pltpu.VMEM((count, wide), F32), jax.ShapeDtypeStruct((16, count), F32)),
        in_specs=[VMEM] * (nb + ni + 4),
        out_specs=(VMEM, VMEM),
        scratch_shapes=[pltpu.VMEM((4, wide, 2 * angles), BF16)],
        compiler_params=params(24),
        cost_estimate=cost(2 * count * wide * 32 * nb * angles, 0),
        name="score",
    )(*blocks, *images, *before, power_pair, prior_rot.reshape(1, count))


def turn_over_kernel(expo_ref, out_ref):
    out_ref[...] = jnp.transpose(expo_ref[...])


def turn_over(expo):
    count, wide = expo.shape
    return pl.pallas_call(
        turn_over_kernel,
        out_shape=pltpu.VMEM((wide, count), F32),
        in_specs=[VMEM],
        out_specs=VMEM,
        compiler_params=params(16),
        cost_estimate=cost(0, 4 * count * wide),
        name="turn_over",
    )(expo)


def share_kernel(expo_ref, own_ref, a_ref, b_ref, c_ref, pair_ref, resp_ref, loglik_ref, denom_ref):
    refs = (own_ref, a_ref, b_ref, c_ref)
    peaks = [ref[0:8] for ref in refs]
    peak = jnp.maximum(jnp.maximum(peaks[0], peaks[1]), jnp.maximum(peaks[2], peaks[3]))
    scales = [jnp.exp(value - peak) for value in peaks]
    total = sum(scale * ref[8:16] for scale, ref in zip(scales, refs))
    loglik_ref[...] = peak + jnp.log(total)
    factor = (scales[0] / total)[0:1]
    resp = (expo_ref[...] * factor).astype(BF16)
    resp_ref[...] = resp
    classes, cycles = denom_ref.shape
    rows = jnp.dot(resp, pair_ref[...], preferred_element_type=F32)
    rows = rows[:, :cycles] + rows[:, cycles:]
    denom = rows[:classes]
    for turn in range(1, ROTS):
        denom = denom + rows[turn * classes : (turn + 1) * classes]
    denom_ref[...] = denom


def share(expo, own, others, power_pair, classes):
    wide, count = expo.shape
    cycles = power_pair.shape[1] // 2
    return pl.pallas_call(
        share_kernel,
        out_shape=(
            pltpu.VMEM((wide, count), BF16),
            jax.ShapeDtypeStruct((8, count), F32),
            pltpu.VMEM((classes, cycles), F32),
        ),
        in_specs=[VMEM] * 6,
        out_specs=(VMEM, VMEM, VMEM),
        compiler_params=params(24),
        name="share",
    )(expo, own, *others, power_pair)


def pack_denom(denom):
    lane = lax.broadcasted_iota(jnp.int32, denom.shape, 1)
    high, low = split2(denom)
    packed = jnp.where(lane < 32, high.astype(F32), pltpu.roll(low.astype(F32), 32, 1))
    return jnp.where(lane < 64, packed, 0.0)


def join_denom(packed):
    lane = lax.broadcasted_iota(jnp.int32, packed.shape, 1)
    return jnp.where(lane < 32, packed + pltpu.roll(packed, 96, 1), 0.0)


def gather_sums(dx, resp, images, denom, dtype):
    classes, cycles = denom.shape
    angles = images[0].shape[2]
    wide, count = resp.shape
    length = 4 * NZ * NY
    ni = len(images)

    def kernel(*refs):
        resp_ref, image_refs = refs[0], refs[1 : 1 + ni]
        denom_ref, out_ref = refs[1 + ni :]
        for j in range(0, length, 2):
            side = jnp.concatenate(
                [
                    jnp.concatenate([ref[cycle_of(dx, j + i)] for ref in image_refs], axis=0)
                    for i in range(2)
                ],
                axis=1,
            )
            sums = jnp.dot(resp_ref[...], side, preferred_element_type=F32)
            for i in range(2):
                total = None
                for turn in range(ROTS):
                    piece = sums[turn * classes : (turn + 1) * classes, i * angles : (i + 1) * angles]
                    if turn:
                        piece = pltpu.roll(piece, angles - 8 * turn, 1)
                    total = piece if total is None else total + piece
                out_ref[j + i] = total.astype(dtype)
        x = lax.axis_index("dom") // (NZ * NY)
        offset = ((x + dx) % NX) * length
        mine = pltpu.roll(denom_ref[...], (cycles - offset) % cycles, 1)
        lane = lax.broadcasted_iota(jnp.int32, mine.shape, 1)
        if dtype == BF16:
            out_ref[length] = pack_denom(mine).astype(BF16)
        else:
            out_ref[length] = jnp.where(lane < length, mine, 0.0)

    return pl.pallas_call(
        kernel,
        out_shape=jax.ShapeDtypeStruct((length + 1, classes, angles), dtype),
        in_specs=[VMEM] * (ni + 2),
        out_specs=VMEM,
        compiler_params=params(24),
        cost_estimate=cost(2 * count * wide * length * angles, 0),
        name="gather_sums",
    )(resp, *images, denom)


def add_parts(own, others, ways):
    rows, classes, angles = own.shape
    length = (rows - 1) // ways

    def kernel(own_ref, *refs):
        others_ref, outs = refs[: len(others)], refs[len(others) :]
        total = own_ref[rows - 1]
        for ref in others_ref:
            total = total + ref[rows - 1].astype(F32)
        denom = join_denom(total)
        packed = pack_denom(denom).astype(BF16)
        for way in range(ways):
            for j in range(length):
                total = own_ref[way * length + j]
                for ref in others_ref:
                    total = total + ref[way * length + j].astype(F32)
                outs[way][j] = total.astype(outs[way].dtype)
            outs[way][length] = packed if way else denom

    shape = (length + 1, classes, angles)
    return pl.pallas_call(
        kernel,
        out_shape=tuple(
            jax.ShapeDtypeStruct(shape, BF16 if way else F32) for way in range(ways)
        ),
        in_specs=[VMEM] * (1 + len(others)),
        out_specs=(VMEM,) * ways,
        compiler_params=params(16),
        cost_estimate=cost(2 * 384 * 512 * 32 * 128, 0),
        name="add_parts",
    )(own, *others)


def finish(own, others):
    rows, classes, angles = own.shape

    def kernel(own_ref, *refs):
        others_ref, out_ref = refs[:-1], refs[-1]
        dom = lax.axis_index("dom")
        offset = ((dom // NY) % NZ) * (4 * NY) + (dom % NY) * 4
        denom = own_ref[rows - 1]
        for ref in others_ref:
            denom = denom + ref[rows - 1].astype(F32)
        denom = pltpu.roll(join_denom(denom), (angles - offset) % angles, 1) + TIKHONOV
        for i in range(rows - 1):
            numer = own_ref[i]
            for ref in others_ref:
                numer = numer + ref[i].astype(F32)
            out_ref[:, i, :] = numer / denom[:, i : i + 1]

    return pl.pallas_call(
        kernel,
        out_shape=jax.ShapeDtypeStruct((classes, rows - 1, angles), F32),
        in_specs=[VMEM] * (1 + len(others)),
        out_specs=VMEM,
        compiler_params=params(16),
        name="finish",
    )(own, *others)


def local(particles, references, ctf_table, noise_inv, groups, prior_rot):
    classes = references.shape[0]
    parts = 4
    particles, ctf_table, noise_inv = (
        pltpu.with_memory_space_constraint(value, pltpu.HBM)
        for value in (particles, ctf_table, noise_inv.reshape(1, -1))
    )
    from_z = send(references, 0, 1, 0)
    weight, power_pair, here = setup(groups, ctf_table, noise_inv, particles, parts)
    piece = join([references, from_z], weight, turned=True)
    from_y = [send(piece, 0, 0, -d) for d in (1, 2, 3)]
    images = []
    for part in range(parts):
        image, token, *rest = weigh(particles, here, weight, part, parts)
        here = rest[0] if rest else None
        images.append(image)
        if part == 1:
            piece = join([piece] + from_y, token)
        if part == 2:
            late = join([piece], token)
    blocks = [piece] + [send(late if d == 2 else piece, -d, 0, 0) for d in (1, 2, 3)]

    before = correlate((0,), blocks[:1], images, None)
    before = correlate((3,), [blocks[3]], images, before)
    before = correlate((1,), [blocks[1]], images, before)
    expo, stats = score((2,), [blocks[2]], images, before, power_pair, prior_rot)
    others = [lax.ppermute(stats, "cls", [(i, i ^ j) for i in range(4)]) for j in (1, 2, 3)]
    turned = turn_over(expo)
    resp, loglik, denom = share(turned, stats, others, power_pair, classes)

    arrived = []
    for d in (2, 1, 3):
        arrived.append(send(gather_sums(d, resp, images, denom, BF16), d, 0, 0))
    own = gather_sums(0, resp, images, denom, F32)
    for value in arrived[:2]:
        (own,) = add_parts(own, [value], 1)
    pieces = add_parts(own, arrived[2:], NY)
    arrived = [send(pieces[d], 0, 0, d) for d in (1, 2, 3)]
    pieces = add_parts(pieces[0], arrived, NZ)
    new_refs = finish(pieces[0], [send(pieces[1], 0, 1, 0)])
    return (new_refs, loglik[0])


def solution(mesh):
    in_specs = (P("dom", None, None), P("cls", "dom", None), P(), P(), P("dom"), P("dom"))
    out_specs = (P("cls", "dom", None), P("dom"))
    return jax.shard_map(local, mesh=mesh, in_specs=in_specs, out_specs=out_specs, check_vma=False)
```

```python
import jax
import jax.numpy as jnp
from jax import lax
from jax.experimental import pallas as pl
from jax.experimental.pallas import tpu as pltpu
from jax.sharding import PartitionSpec as P

ROTS = 16
PRIOR_WEIGHT = 0.02
TIKHONOV = 1.0
F32 = jnp.float32
BF16 = jnp.bfloat16
NX, NZ, NY = 4, 2, 4
VMEM = pl.BlockSpec(memory_space=pltpu.VMEM)
HBM = pl.BlockSpec(memory_space=pltpu.HBM)
MIB = 2**20
STREAMS = 1


def params(mib):
    return pltpu.CompilerParams(vmem_limit_bytes=mib * MIB)


def cost(flops, nbytes):
    return pl.CostEstimate(flops=flops // 64, bytes_accessed=nbytes // 64, transcendentals=0)


def coords(i):
    return i // (NZ * NY), (i // NY) % NZ, i % NY


def shift(dx, dz, dy):
    pairs = []
    for i in range(NX * NZ * NY):
        x, z, y = coords(i)
        pairs.append((i, ((x + dx) % NX) * NZ * NY + ((z + dz) % NZ) * NY + (y + dy) % NY))
    return pairs


def send(value, dx, dz, dy):
    return lax.ppermute(value, "dom", shift(dx, dz, dy))


def split2(value):
    high = value.astype(BF16)
    low = (value - high.astype(F32)).astype(BF16)
    return high, low


def load_rows(source, start, target, sems, first):
    rows = target.shape[0] // STREAMS
    return [
        pltpu.make_async_copy(
            source.at[pl.ds(start + i * rows, rows)], target.at[pl.ds(i * rows, rows)], sems.at[first + i]
        )
        for i in range(STREAMS)
    ]


def setup_kernel(groups_ref, ctf_hbm, noise_hbm, particles_hbm, weight_ref, power_ref, first_ref, ctf_ref, noise_ref, sems):
    count = groups_ref.shape[0]
    group_count, cycles = ctf_ref.shape
    copies = [
        pltpu.make_async_copy(ctf_hbm, ctf_ref, sems.at[0]),
        pltpu.make_async_copy(noise_hbm, noise_ref, sems.at[1]),
    ]
    copies += load_rows(particles_hbm, 0, first_ref, sems, 2)
    for copy in copies:
        copy.start()
    choose = (
        lax.broadcasted_iota(jnp.int32, (group_count, count), 0) == groups_ref[...].reshape(1, count)
    ).astype(F32)
    pick = lambda table: lax.dot_general(
        choose, table, (((0,), (0,)), ((), ())), precision=lax.Precision.HIGHEST,
        preferred_element_type=F32,
    )
    copies[0].wait()
    copies[1].wait()
    ctf = ctf_ref[...]
    noise = noise_ref[...]
    weight_ref[...] = pick(ctf) * noise
    high, low = split2(pick(ctf * ctf * noise))
    power_ref[:, :cycles] = high
    power_ref[:, cycles:] = low
    for copy in copies[2:]:
        copy.wait()


def setup(groups, ctf_table, noise_inv, particles, parts):
    count = groups.shape[0]
    cycles = ctf_table.shape[1]
    return pl.pallas_call(
        setup_kernel,
        out_shape=(
            jax.ShapeDtypeStruct((count, cycles), F32),
            jax.ShapeDtypeStruct((count, 2 * cycles), BF16),
            pltpu.VMEM((count // parts,) + particles.shape[1:], BF16),
        ),
        in_specs=[VMEM, HBM, HBM, HBM],
        out_specs=(VMEM, VMEM, VMEM),
        scratch_shapes=[
            pltpu.VMEM(ctf_table.shape, F32),
            pltpu.VMEM((1, cycles), F32),
            pltpu.SemaphoreType.DMA((2 + STREAMS,)),
        ],
        compiler_params=params(16),
        name="setup",
    )(groups, ctf_table, noise_inv, particles)


def weigh(particles, here, weight, part, parts):
    count, cycles, angles = particles.shape
    rows = count // parts
    pitch = cycles + 1
    last = part == parts - 1

    def kernel(particles_hbm, here_ref, weight_ref, out_ref, token_ref, *refs):
        if not last:
            next_ref, wide, sems = refs
            copies = load_rows(particles_hbm, (part + 1) * rows, next_ref, sems, 0)
            for copy in copies:
                copy.start()
        else:
            wide = refs[0]
        values = weight_ref[part * rows : (part + 1) * rows]
        token_ref[...] = values[0:8]
        for n in range(rows):
            wide[pl.ds(n * pitch, cycles), :] = here_ref[n].astype(F32)
        pair = jnp.concatenate(split2(values), axis=1)
        row = lax.broadcasted_iota(jnp.int32, (16, 2 * angles), 0)
        side = lax.broadcasted_iota(jnp.int32, (16, 2 * angles), 1) // angles
        for q in range(0, cycles, 2):
            if q % 6 < 4:
                base = q // 16 * 16
                pick = [jnp.where(row - side == q % 16, 1.0, 0.0).astype(BF16)]
                if base:
                    pick = [jnp.zeros((base, 2 * angles), BF16)] + pick
                if base + 16 < cycles:
                    pick = pick + [jnp.zeros((cycles - 16 - base, 2 * angles), BF16)]
                spread = jnp.dot(
                    pair, jnp.concatenate(pick * 2, axis=0), preferred_element_type=F32
                )
                scales = [spread[:, :angles], spread[:, angles:]]
            else:
                scales = [values[:, q : q + 1], values[:, q + 1 : q + 2]]
            for i in range(2):
                image = wide[pl.ds(q + i, rows, stride=pitch), :]
                out_ref[q + i] = (image * scales[i]).astype(BF16)
        if not last:
            for copy in copies:
                copy.wait()

    shape = (rows, cycles, angles)
    return pl.pallas_call(
        kernel,
        out_shape=(pltpu.VMEM((cycles, rows, angles), BF16), jax.ShapeDtypeStruct((8, cycles), F32))
        + (() if last else (pltpu.VMEM(shape, BF16),)),
        in_specs=[HBM, VMEM, VMEM],
        out_specs=(VMEM,) * (2 if last else 3),
        scratch_shapes=[pltpu.VMEM((rows * pitch + 8, angles), F32)]
        + ([] if last else [pltpu.SemaphoreType.DMA((STREAMS,))]),
        compiler_params=params(16),
        cost_estimate=cost(0, rows * cycles * angles * 16),
        name="weigh",
    )(particles, here, weight)


def join(pieces, *tokens, turned=False):
    rows, classes, angles = pieces[0].shape
    if turned:
        rows, classes = classes, rows

    def kernel(*refs):
        out_ref = refs[-1]
        for i, ref in enumerate(refs[: len(pieces)]):
            for j in range(rows):
                out_ref[i * rows + j] = ref[:, j, :] if turned else ref[j]

    return pl.pallas_call(
        kernel,
        out_shape=jax.ShapeDtypeStruct((rows * len(pieces), classes, angles), BF16),
        in_specs=[VMEM] * len(pieces) + [pl.BlockSpec(memory_space=pl.ANY)] * len(tokens),
        out_specs=VMEM,
        compiler_params=params(16),
        name="join",
    )(*pieces, *tokens)


def cycle_of(dx, j):
    dom = lax.axis_index("dom")
    x, z, y = dom // (NZ * NY), (dom // NY) % NZ, dom % NY
    dy, dz, i = j // (4 * NZ), (j // 4) % NZ, j % 4
    return ((x + dx) % NX) * (4 * NZ * NY) + ((z + dz) % NZ) * (4 * NY) + ((y + dy) % NY) * 4 + i


def correlate_steps(shifts, block_refs, image_refs, turned, total, power):
    classes, angles = block_refs[0].shape[1:]
    lane = lax.broadcasted_iota(jnp.int32, power.shape, 1)
    slot = 0
    for dx, block_ref in zip(shifts, block_refs):
        for j in range(0, block_ref.shape[0], 2):
            sides = []
            for i in range(2):
                piece = block_ref[j + i]
                cycle = cycle_of(dx, j + i)
                for turn in range(ROTS):
                    turned[slot % 4, turn * classes : (turn + 1) * classes, i * angles : (i + 1) * angles] = (
                        pltpu.roll(piece, 8 * turn, 1) if turn else piece
                    )
                wide = piece.astype(F32)
                power = jnp.where(lane == cycle, jnp.sum(wide * wide, axis=1, keepdims=True), power)
                sides.append(jnp.concatenate([ref[cycle] for ref in image_refs], axis=0))
            part = lax.dot_general(
                jnp.concatenate(sides, axis=1), turned[slot % 4], (((1,), (1,)), ((), ())),
                preferred_element_type=F32,
            )
            total = part if total is None else total + part
            slot += 1
    return total, power


def correlate(shifts, blocks, images, before):
    cycles = images[0].shape[0]
    angles = images[0].shape[2]
    count = sum(image.shape[1] for image in images)
    classes = blocks[0].shape[1]
    wide = ROTS * classes
    nb, ni = len(blocks), len(images)

    def kernel(*refs):
        block_refs, image_refs = refs[:nb], refs[nb : nb + ni]
        rest = refs[nb + ni :]
        if before is not None:
            total, power = rest[0][...], rest[1][...]
            rest = rest[2:]
        else:
            total, power = None, jnp.zeros((classes, cycles), F32)
        total_ref, power_ref, turned = rest
        total, power = correlate_steps(shifts, block_refs, image_refs, turned, total, power)
        total_ref[...] = total
        power_ref[...] = power

    extra = [] if before is None else list(before)
    return pl.pallas_call(
        kernel,
        out_shape=(pltpu.VMEM((count, wide), F32), pltpu.VMEM((classes, cycles), F32)),
        in_specs=[VMEM] * (nb + ni + len(extra)),
        out_specs=(VMEM, VMEM),
        scratch_shapes=[pltpu.VMEM((4, wide, 2 * angles), BF16)],
        compiler_params=params(24),
        cost_estimate=cost(2 * count * wide * 32 * nb * angles, 0),
        name="correlate",
    )(*blocks, *images, *extra)


def score(shifts, blocks, images, before, power_pair, prior_rot):
    cycles = images[0].shape[0]
    angles = images[0].shape[2]
    count = sum(image.shape[1] for image in images)
    classes = blocks[0].shape[1]
    wide = ROTS * classes
    nb, ni = len(blocks), len(images)

    def kernel(*refs):
        block_refs, image_refs = refs[:nb], refs[nb : nb + ni]
        total_ref, cycle_ref, pair_ref, prior_ref, expo_ref, stats_ref, turned = refs[nb + ni :]
        total, power = correlate_steps(
            shifts, block_refs, image_refs, turned, total_ref[...], cycle_ref[...]
        )
        high, low = split2(-0.5 * power)
        both = jnp.concatenate([high, high], axis=1)
        low_both = jnp.concatenate([low, low], axis=1)
        pair = pair_ref[...]
        norm = lax.dot_general(pair, both, (((1,), (1,)), ((), ())), preferred_element_type=F32)
        norm = norm + lax.dot_general(
            pair, low_both, (((1,), (1,)), ((), ())), preferred_element_type=F32
        )
        total = total + jnp.concatenate([norm] * ROTS, axis=1)
        hot = (
            lax.broadcasted_iota(jnp.int32, (2 * ROTS, count), 0) % ROTS == prior_ref[...]
        ).astype(BF16)
        row = lax.broadcasted_iota(jnp.int32, (2 * ROTS, wide), 0)
        turn = lax.broadcasted_iota(jnp.int32, (2 * ROTS, wide), 1) // classes
        offset = (turn - row + 2 * ROTS) % ROTS
        distance = jnp.minimum(offset, ROTS - offset).astype(F32)
        prior = -PRIOR_WEIGHT * distance * distance
        high, low = split2(prior)
        table = jnp.where(row < ROTS, high.astype(F32), low.astype(F32)).astype(BF16)
        total = total + lax.dot_general(
            hot, table, (((0,), (0,)), ((), ())), preferred_element_type=F32
        )
        peak = jnp.max(total, axis=1, keepdims=True)
        expo = jnp.exp(total - peak)
        expo_ref[...] = expo
        mass = jnp.sum(expo, axis=1, keepdims=True)
        lane = lax.broadcasted_iota(jnp.int32, (count, 128), 1)
        stats = jnp.transpose(jnp.where(lane < 64, peak, mass))
        stats_ref[0:8] = stats[0:8]
        stats_ref[8:16] = stats[64:72]

    return pl.pallas_call(
        kernel,
        out_shape=(pltpu.VMEM((count, wide), F32), jax.ShapeDtypeStruct((16, count), F32)),
        in_specs=[VMEM] * (nb + ni + 4),
        out_specs=(VMEM, VMEM),
        scratch_shapes=[pltpu.VMEM((4, wide, 2 * angles), BF16)],
        compiler_params=params(24),
        cost_estimate=cost(2 * count * wide * 32 * nb * angles, 0),
        name="score",
    )(*blocks, *images, *before, power_pair, prior_rot.reshape(1, count))


def turn_over_kernel(expo_ref, out_ref):
    out_ref[...] = jnp.transpose(expo_ref[...])


def turn_over(expo):
    count, wide = expo.shape
    return pl.pallas_call(
        turn_over_kernel,
        out_shape=pltpu.VMEM((wide, count), F32),
        in_specs=[VMEM],
        out_specs=VMEM,
        compiler_params=params(16),
        cost_estimate=cost(0, 4 * count * wide),
        name="turn_over",
    )(expo)


def share_kernel(expo_ref, own_ref, a_ref, b_ref, c_ref, pair_ref, resp_ref, loglik_ref, denom_ref):
    refs = (own_ref, a_ref, b_ref, c_ref)
    peaks = [ref[0:8] for ref in refs]
    peak = jnp.maximum(jnp.maximum(peaks[0], peaks[1]), jnp.maximum(peaks[2], peaks[3]))
    scales = [jnp.exp(value - peak) for value in peaks]
    total = sum(scale * ref[8:16] for scale, ref in zip(scales, refs))
    loglik_ref[...] = peak + jnp.log(total)
    factor = (scales[0] / total)[0:1]
    resp = (expo_ref[...] * factor).astype(BF16)
    resp_ref[...] = resp
    classes, cycles = denom_ref.shape
    rows = jnp.dot(resp, pair_ref[...], preferred_element_type=F32)
    rows = rows[:, :cycles] + rows[:, cycles:]
    denom = rows[:classes]
    for turn in range(1, ROTS):
        denom = denom + rows[turn * classes : (turn + 1) * classes]
    denom_ref[...] = denom


def share(expo, own, others, power_pair, classes):
    wide, count = expo.shape
    cycles = power_pair.shape[1] // 2
    return pl.pallas_call(
        share_kernel,
        out_shape=(
            pltpu.VMEM((wide, count), BF16),
            jax.ShapeDtypeStruct((8, count), F32),
            pltpu.VMEM((classes, cycles), F32),
        ),
        in_specs=[VMEM] * 6,
        out_specs=(VMEM, VMEM, VMEM),
        compiler_params=params(24),
        name="share",
    )(expo, own, *others, power_pair)


def pack_denom(denom):
    lane = lax.broadcasted_iota(jnp.int32, denom.shape, 1)
    high, low = split2(denom)
    packed = jnp.where(lane < 32, high.astype(F32), pltpu.roll(low.astype(F32), 32, 1))
    return jnp.where(lane < 64, packed, 0.0)


def join_denom(packed):
    lane = lax.broadcasted_iota(jnp.int32, packed.shape, 1)
    return jnp.where(lane < 32, packed + pltpu.roll(packed, 96, 1), 0.0)


def gather_sums(dx, resp, images, denom, dtype):
    classes, cycles = denom.shape
    angles = images[0].shape[2]
    wide, count = resp.shape
    length = 4 * NZ * NY
    ni = len(images)

    def kernel(*refs):
        resp_ref, image_refs = refs[0], refs[1 : 1 + ni]
        denom_ref, out_ref = refs[1 + ni :]
        for j in range(0, length, 2):
            side = jnp.concatenate(
                [
                    jnp.concatenate([ref[cycle_of(dx, j + i)] for ref in image_refs], axis=0)
                    for i in range(2)
                ],
                axis=1,
            )
            sums = jnp.dot(resp_ref[...], side, preferred_element_type=F32)
            for i in range(2):
                total = None
                for turn in range(ROTS):
                    piece = sums[turn * classes : (turn + 1) * classes, i * angles : (i + 1) * angles]
                    if turn:
                        piece = pltpu.roll(piece, angles - 8 * turn, 1)
                    total = piece if total is None else total + piece
                out_ref[j + i] = total.astype(dtype)
        x = lax.axis_index("dom") // (NZ * NY)
        offset = ((x + dx) % NX) * length
        mine = pltpu.roll(denom_ref[...], (cycles - offset) % cycles, 1)
        lane = lax.broadcasted_iota(jnp.int32, mine.shape, 1)
        if dtype == BF16:
            out_ref[length] = pack_denom(mine).astype(BF16)
        else:
            out_ref[length] = jnp.where(lane < length, mine, 0.0)

    return pl.pallas_call(
        kernel,
        out_shape=jax.ShapeDtypeStruct((length + 1, classes, angles), dtype),
        in_specs=[VMEM] * (ni + 2),
        out_specs=VMEM,
        compiler_params=params(24),
        cost_estimate=cost(2 * count * wide * length * angles, 0),
        name="gather_sums",
    )(resp, *images, denom)


def add_parts(own, others, ways):
    rows, classes, angles = own.shape
    length = (rows - 1) // ways

    def kernel(own_ref, *refs):
        others_ref, outs = refs[: len(others)], refs[len(others) :]
        total = own_ref[rows - 1]
        for ref in others_ref:
            total = total + ref[rows - 1].astype(F32)
        denom = join_denom(total)
        packed = pack_denom(denom).astype(BF16)
        for way in range(ways):
            for j in range(length):
                total = own_ref[way * length + j]
                for ref in others_ref:
                    total = total + ref[way * length + j].astype(F32)
                outs[way][j] = total.astype(outs[way].dtype)
            outs[way][length] = packed if way else denom

    shape = (length + 1, classes, angles)
    return pl.pallas_call(
        kernel,
        out_shape=tuple(
            jax.ShapeDtypeStruct(shape, BF16 if way else F32) for way in range(ways)
        ),
        in_specs=[VMEM] * (1 + len(others)),
        out_specs=(VMEM,) * ways,
        compiler_params=params(16),
        cost_estimate=cost(2 * 384 * 512 * 32 * 128, 0),
        name="add_parts",
    )(own, *others)


def finish(own, others):
    rows, classes, angles = own.shape

    def kernel(own_ref, *refs):
        others_ref, out_ref = refs[:-1], refs[-1]
        dom = lax.axis_index("dom")
        offset = ((dom // NY) % NZ) * (4 * NY) + (dom % NY) * 4
        denom = own_ref[rows - 1]
        for ref in others_ref:
            denom = denom + ref[rows - 1].astype(F32)
        denom = pltpu.roll(join_denom(denom), (angles - offset) % angles, 1) + TIKHONOV
        for i in range(rows - 1):
            numer = own_ref[i]
            for ref in others_ref:
                numer = numer + ref[i].astype(F32)
            out_ref[:, i, :] = numer / denom[:, i : i + 1]

    return pl.pallas_call(
        kernel,
        out_shape=jax.ShapeDtypeStruct((classes, rows - 1, angles), F32),
        in_specs=[VMEM] * (1 + len(others)),
        out_specs=VMEM,
        compiler_params=params(16),
        name="finish",
    )(own, *others)


def local(particles, references, ctf_table, noise_inv, groups, prior_rot):
    classes = references.shape[0]
    parts = 4
    particles, ctf_table, noise_inv = (
        pltpu.with_memory_space_constraint(value, pltpu.HBM)
        for value in (particles, ctf_table, noise_inv.reshape(1, -1))
    )
    from_z = send(references, 0, 1, 0)
    weight, power_pair, here = setup(groups, ctf_table, noise_inv, particles, parts)
    piece = join([references, from_z], weight, turned=True)
    from_y = [send(piece, 0, 0, -d) for d in (1, 2, 3)]
    images = []
    for part in range(parts):
        image, token, *rest = weigh(particles, here, weight, part, parts)
        here = rest[0] if rest else None
        images.append(image)
        if part == 1:
            piece = join([piece] + from_y, token)
        if part == 2:
            late = join([piece], token)
    blocks = [piece] + [send(late if d == 1 else piece, -d, 0, 0) for d in (1, 2, 3)]

    before = correlate((0,), blocks[:1], images, None)
    before = correlate((3,), [blocks[3]], images, before)
    before = correlate((2,), [blocks[2]], images, before)
    expo, stats = score((1,), [blocks[1]], images, before, power_pair, prior_rot)
    others = [lax.ppermute(stats, "cls", [(i, i ^ j) for i in range(4)]) for j in (1, 2, 3)]
    turned = turn_over(expo)
    resp, loglik, denom = share(turned, stats, others, power_pair, classes)

    arrived = []
    for d in (2, 1, 3):
        arrived.append(send(gather_sums(d, resp, images, denom, BF16), d, 0, 0))
    own = gather_sums(0, resp, images, denom, F32)
    for value in arrived[:2]:
        (own,) = add_parts(own, [value], 1)
    pieces = add_parts(own, arrived[2:], NY)
    arrived = [send(pieces[d], 0, 0, d) for d in (1, 2, 3)]
    pieces = add_parts(pieces[0], arrived, NZ)
    new_refs = finish(pieces[0], [send(pieces[1], 0, 1, 0)])
    return (new_refs, loglik[0])


def solution(mesh):
    in_specs = (P("dom", None, None), P("cls", "dom", None), P(), P(), P("dom"), P("dom"))
    out_specs = (P("cls", "dom", None), P("dom"))
    return jax.shard_map(local, mesh=mesh, in_specs=in_specs, out_specs=out_specs, check_vma=False)
```

```python
import jax
import jax.numpy as jnp
from jax import lax
from jax.experimental import pallas as pl
from jax.experimental.pallas import tpu as pltpu
from jax.sharding import PartitionSpec as P

ROTS = 16
PRIOR_WEIGHT = 0.02
TIKHONOV = 1.0
F32 = jnp.float32
BF16 = jnp.bfloat16
NX, NZ, NY = 4, 2, 4
VMEM = pl.BlockSpec(memory_space=pltpu.VMEM)
HBM = pl.BlockSpec(memory_space=pltpu.HBM)
MIB = 2**20
STREAMS = 1


def params(mib):
    return pltpu.CompilerParams(vmem_limit_bytes=mib * MIB)


def cost(flops, nbytes):
    return pl.CostEstimate(flops=flops // 64, bytes_accessed=nbytes // 64, transcendentals=0)


def coords(i):
    return i // (NZ * NY), (i // NY) % NZ, i % NY


def shift(dx, dz, dy):
    pairs = []
    for i in range(NX * NZ * NY):
        x, z, y = coords(i)
        pairs.append((i, ((x + dx) % NX) * NZ * NY + ((z + dz) % NZ) * NY + (y + dy) % NY))
    return pairs


def send(value, dx, dz, dy):
    return lax.ppermute(value, "dom", shift(dx, dz, dy))


def split2(value):
    high = value.astype(BF16)
    low = (value - high.astype(F32)).astype(BF16)
    return high, low


def load_rows(source, start, target, sems, first):
    rows = target.shape[0] // STREAMS
    return [
        pltpu.make_async_copy(
            source.at[pl.ds(start + i * rows, rows)], target.at[pl.ds(i * rows, rows)], sems.at[first + i]
        )
        for i in range(STREAMS)
    ]


def setup_kernel(groups_ref, ctf_hbm, noise_hbm, particles_hbm, weight_ref, power_ref, first_ref, ctf_ref, noise_ref, sems):
    count = groups_ref.shape[0]
    group_count, cycles = ctf_ref.shape
    copies = [
        pltpu.make_async_copy(ctf_hbm, ctf_ref, sems.at[0]),
        pltpu.make_async_copy(noise_hbm, noise_ref, sems.at[1]),
    ]
    copies += load_rows(particles_hbm, 0, first_ref, sems, 2)
    for copy in copies:
        copy.start()
    choose = (
        lax.broadcasted_iota(jnp.int32, (group_count, count), 0) == groups_ref[...].reshape(1, count)
    ).astype(F32)
    pick = lambda table: lax.dot_general(
        choose, table, (((0,), (0,)), ((), ())), precision=lax.Precision.HIGHEST,
        preferred_element_type=F32,
    )
    copies[0].wait()
    copies[1].wait()
    ctf = ctf_ref[...]
    noise = noise_ref[...]
    weight_ref[...] = pick(ctf) * noise
    high, low = split2(pick(ctf * ctf * noise))
    power_ref[:, :cycles] = high
    power_ref[:, cycles:] = low
    for copy in copies[2:]:
        copy.wait()


def setup(groups, ctf_table, noise_inv, particles, parts):
    count = groups.shape[0]
    cycles = ctf_table.shape[1]
    return pl.pallas_call(
        setup_kernel,
        out_shape=(
            jax.ShapeDtypeStruct((count, cycles), F32),
            jax.ShapeDtypeStruct((count, 2 * cycles), BF16),
            pltpu.VMEM((count // parts,) + particles.shape[1:], BF16),
        ),
        in_specs=[VMEM, HBM, HBM, HBM],
        out_specs=(VMEM, VMEM, VMEM),
        scratch_shapes=[
            pltpu.VMEM(ctf_table.shape, F32),
            pltpu.VMEM((1, cycles), F32),
            pltpu.SemaphoreType.DMA((2 + STREAMS,)),
        ],
        compiler_params=params(16),
        name="setup",
    )(groups, ctf_table, noise_inv, particles)


def weigh(particles, here, weight, part, parts):
    count, cycles, angles = particles.shape
    rows = count // parts
    pitch = cycles + 1
    last = part == parts - 1

    def kernel(particles_hbm, here_ref, weight_ref, out_ref, token_ref, *refs):
        if not last:
            next_ref, wide, sems = refs
            copies = load_rows(particles_hbm, (part + 1) * rows, next_ref, sems, 0)
            for copy in copies:
                copy.start()
        else:
            wide = refs[0]
        values = weight_ref[part * rows : (part + 1) * rows]
        token_ref[...] = values[0:8]
        for n in range(rows):
            wide[pl.ds(n * pitch, cycles), :] = here_ref[n].astype(F32)
        pair = jnp.concatenate(split2(values), axis=1)
        row = lax.broadcasted_iota(jnp.int32, (16, 2 * angles), 0)
        side = lax.broadcasted_iota(jnp.int32, (16, 2 * angles), 1) // angles
        for q in range(0, cycles, 2):
            if q % 6 < 4:
                base = q // 16 * 16
                pick = [jnp.where(row - side == q % 16, 1.0, 0.0).astype(BF16)]
                if base:
                    pick = [jnp.zeros((base, 2 * angles), BF16)] + pick
                if base + 16 < cycles:
                    pick = pick + [jnp.zeros((cycles - 16 - base, 2 * angles), BF16)]
                spread = jnp.dot(
                    pair, jnp.concatenate(pick * 2, axis=0), preferred_element_type=F32
                )
                scales = [spread[:, :angles], spread[:, angles:]]
            else:
                scales = [values[:, q : q + 1], values[:, q + 1 : q + 2]]
            for i in range(2):
                image = wide[pl.ds(q + i, rows, stride=pitch), :]
                out_ref[q + i] = (image * scales[i]).astype(BF16)
        if not last:
            for copy in copies:
                copy.wait()

    shape = (rows, cycles, angles)
    return pl.pallas_call(
        kernel,
        out_shape=(pltpu.VMEM((cycles, rows, angles), BF16), jax.ShapeDtypeStruct((8, cycles), F32))
        + (() if last else (pltpu.VMEM(shape, BF16),)),
        in_specs=[HBM, VMEM, VMEM],
        out_specs=(VMEM,) * (2 if last else 3),
        scratch_shapes=[pltpu.VMEM((rows * pitch + 8, angles), F32)]
        + ([] if last else [pltpu.SemaphoreType.DMA((STREAMS,))]),
        compiler_params=params(16),
        cost_estimate=cost(0, rows * cycles * angles * 16),
        name="weigh",
    )(particles, here, weight)


def join(pieces, *tokens, turned=False):
    rows, classes, angles = pieces[0].shape
    if turned:
        rows, classes = classes, rows

    def kernel(*refs):
        out_ref = refs[-1]
        for i, ref in enumerate(refs[: len(pieces)]):
            block = ref[...].astype(F32) if turned else None
            for j in range(rows):
                out_ref[i * rows + j] = block[:, j, :].astype(BF16) if turned else ref[j]

    return pl.pallas_call(
        kernel,
        out_shape=jax.ShapeDtypeStruct((rows * len(pieces), classes, angles), BF16),
        in_specs=[VMEM] * len(pieces) + [pl.BlockSpec(memory_space=pl.ANY)] * len(tokens),
        out_specs=VMEM,
        compiler_params=params(16),
        name="join",
    )(*pieces, *tokens)


def cycle_of(dx, j):
    dom = lax.axis_index("dom")
    x, z, y = dom // (NZ * NY), (dom // NY) % NZ, dom % NY
    dy, dz, i = j // (4 * NZ), (j // 4) % NZ, j % 4
    return ((x + dx) % NX) * (4 * NZ * NY) + ((z + dz) % NZ) * (4 * NY) + ((y + dy) % NY) * 4 + i


def correlate_steps(shifts, block_refs, image_refs, turned, total, power):
    classes, angles = block_refs[0].shape[1:]
    lane = lax.broadcasted_iota(jnp.int32, power.shape, 1)
    slot = 0
    for dx, block_ref in zip(shifts, block_refs):
        for j in range(0, block_ref.shape[0], 2):
            sides = []
            for i in range(2):
                piece = block_ref[j + i]
                cycle = cycle_of(dx, j + i)
                for turn in range(ROTS):
                    turned[slot % 4, turn * classes : (turn + 1) * classes, i * angles : (i + 1) * angles] = (
                        pltpu.roll(piece, 8 * turn, 1) if turn else piece
                    )
                wide = piece.astype(F32)
                power = jnp.where(lane == cycle, jnp.sum(wide * wide, axis=1, keepdims=True), power)
                sides.append(jnp.concatenate([ref[cycle] for ref in image_refs], axis=0))
            part = lax.dot_general(
                jnp.concatenate(sides, axis=1), turned[slot % 4], (((1,), (1,)), ((), ())),
                preferred_element_type=F32,
            )
            total = part if total is None else total + part
            slot += 1
    return total, power


def correlate(shifts, blocks, images, before):
    cycles = images[0].shape[0]
    angles = images[0].shape[2]
    count = sum(image.shape[1] for image in images)
    classes = blocks[0].shape[1]
    wide = ROTS * classes
    nb, ni = len(blocks), len(images)

    def kernel(*refs):
        block_refs, image_refs = refs[:nb], refs[nb : nb + ni]
        rest = refs[nb + ni :]
        if before is not None:
            total, power = rest[0][...], rest[1][...]
            rest = rest[2:]
        else:
            total, power = None, jnp.zeros((classes, cycles), F32)
        total_ref, power_ref, turned = rest
        total, power = correlate_steps(shifts, block_refs, image_refs, turned, total, power)
        total_ref[...] = total
        power_ref[...] = power

    extra = [] if before is None else list(before)
    return pl.pallas_call(
        kernel,
        out_shape=(pltpu.VMEM((count, wide), F32), pltpu.VMEM((classes, cycles), F32)),
        in_specs=[VMEM] * (nb + ni + len(extra)),
        out_specs=(VMEM, VMEM),
        scratch_shapes=[pltpu.VMEM((4, wide, 2 * angles), BF16)],
        compiler_params=params(24),
        cost_estimate=cost(2 * count * wide * 32 * nb * angles, 0),
        name="correlate",
    )(*blocks, *images, *extra)


def score(shifts, blocks, images, before, power_pair, prior_rot):
    cycles = images[0].shape[0]
    angles = images[0].shape[2]
    count = sum(image.shape[1] for image in images)
    classes = blocks[0].shape[1]
    wide = ROTS * classes
    nb, ni = len(blocks), len(images)

    def kernel(*refs):
        block_refs, image_refs = refs[:nb], refs[nb : nb + ni]
        total_ref, cycle_ref, pair_ref, prior_ref, expo_ref, stats_ref, turned = refs[nb + ni :]
        total, power = correlate_steps(
            shifts, block_refs, image_refs, turned, total_ref[...], cycle_ref[...]
        )
        high, low = split2(-0.5 * power)
        both = jnp.concatenate([high, high], axis=1)
        low_both = jnp.concatenate([low, low], axis=1)
        pair = pair_ref[...]
        norm = lax.dot_general(pair, both, (((1,), (1,)), ((), ())), preferred_element_type=F32)
        norm = norm + lax.dot_general(
            pair, low_both, (((1,), (1,)), ((), ())), preferred_element_type=F32
        )
        total = total + jnp.concatenate([norm] * ROTS, axis=1)
        hot = (
            lax.broadcasted_iota(jnp.int32, (2 * ROTS, count), 0) % ROTS == prior_ref[...]
        ).astype(BF16)
        row = lax.broadcasted_iota(jnp.int32, (2 * ROTS, wide), 0)
        turn = lax.broadcasted_iota(jnp.int32, (2 * ROTS, wide), 1) // classes
        offset = (turn - row + 2 * ROTS) % ROTS
        distance = jnp.minimum(offset, ROTS - offset).astype(F32)
        prior = -PRIOR_WEIGHT * distance * distance
        high, low = split2(prior)
        table = jnp.where(row < ROTS, high.astype(F32), low.astype(F32)).astype(BF16)
        total = total + lax.dot_general(
            hot, table, (((0,), (0,)), ((), ())), preferred_element_type=F32
        )
        peak = jnp.max(total, axis=1, keepdims=True)
        expo = jnp.exp(total - peak)
        expo_ref[...] = expo
        mass = jnp.sum(expo, axis=1, keepdims=True)
        lane = lax.broadcasted_iota(jnp.int32, (count, 128), 1)
        stats = jnp.transpose(jnp.where(lane < 64, peak, mass))
        stats_ref[0:8] = stats[0:8]
        stats_ref[8:16] = stats[64:72]

    return pl.pallas_call(
        kernel,
        out_shape=(pltpu.VMEM((count, wide), F32), jax.ShapeDtypeStruct((16, count), F32)),
        in_specs=[VMEM] * (nb + ni + 4),
        out_specs=(VMEM, VMEM),
        scratch_shapes=[pltpu.VMEM((4, wide, 2 * angles), BF16)],
        compiler_params=params(24),
        cost_estimate=cost(2 * count * wide * 32 * nb * angles, 0),
        name="score",
    )(*blocks, *images, *before, power_pair, prior_rot.reshape(1, count))


def turn_over_kernel(expo_ref, out_ref):
    out_ref[...] = jnp.transpose(expo_ref[...])


def turn_over(expo):
    count, wide = expo.shape
    return pl.pallas_call(
        turn_over_kernel,
        out_shape=pltpu.VMEM((wide, count), F32),
        in_specs=[VMEM],
        out_specs=VMEM,
        compiler_params=params(16),
        cost_estimate=cost(0, 4 * count * wide),
        name="turn_over",
    )(expo)


def share_kernel(expo_ref, own_ref, a_ref, b_ref, c_ref, pair_ref, resp_ref, loglik_ref, denom_ref):
    refs = (own_ref, a_ref, b_ref, c_ref)
    peaks = [ref[0:8] for ref in refs]
    peak = jnp.maximum(jnp.maximum(peaks[0], peaks[1]), jnp.maximum(peaks[2], peaks[3]))
    scales = [jnp.exp(value - peak) for value in peaks]
    total = sum(scale * ref[8:16] for scale, ref in zip(scales, refs))
    loglik_ref[...] = peak + jnp.log(total)
    factor = (scales[0] / total)[0:1]
    resp = (expo_ref[...] * factor).astype(BF16)
    resp_ref[...] = resp
    classes, cycles = denom_ref.shape
    rows = jnp.dot(resp, pair_ref[...], preferred_element_type=F32)
    rows = rows[:, :cycles] + rows[:, cycles:]
    denom = rows[:classes]
    for turn in range(1, ROTS):
        denom = denom + rows[turn * classes : (turn + 1) * classes]
    denom_ref[...] = denom


def share(expo, own, others, power_pair, classes):
    wide, count = expo.shape
    cycles = power_pair.shape[1] // 2
    return pl.pallas_call(
        share_kernel,
        out_shape=(
            pltpu.VMEM((wide, count), BF16),
            jax.ShapeDtypeStruct((8, count), F32),
            pltpu.VMEM((classes, cycles), F32),
        ),
        in_specs=[VMEM] * 6,
        out_specs=(VMEM, VMEM, VMEM),
        compiler_params=params(24),
        name="share",
    )(expo, own, *others, power_pair)


def pack_denom(denom):
    lane = lax.broadcasted_iota(jnp.int32, denom.shape, 1)
    high, low = split2(denom)
    packed = jnp.where(lane < 32, high.astype(F32), pltpu.roll(low.astype(F32), 32, 1))
    return jnp.where(lane < 64, packed, 0.0)


def join_denom(packed):
    lane = lax.broadcasted_iota(jnp.int32, packed.shape, 1)
    return jnp.where(lane < 32, packed + pltpu.roll(packed, 96, 1), 0.0)


def gather_sums(dx, resp, images, denom, dtype):
    classes, cycles = denom.shape
    angles = images[0].shape[2]
    wide, count = resp.shape
    length = 4 * NZ * NY
    ni = len(images)

    def kernel(*refs):
        resp_ref, image_refs = refs[0], refs[1 : 1 + ni]
        denom_ref, out_ref = refs[1 + ni :]
        for j in range(0, length, 2):
            side = jnp.concatenate(
                [
                    jnp.concatenate([ref[cycle_of(dx, j + i)] for ref in image_refs], axis=0)
                    for i in range(2)
                ],
                axis=1,
            )
            sums = jnp.dot(resp_ref[...], side, preferred_element_type=F32)
            for i in range(2):
                total = None
                for turn in range(ROTS):
                    piece = sums[turn * classes : (turn + 1) * classes, i * angles : (i + 1) * angles]
                    if turn:
                        piece = pltpu.roll(piece, angles - 8 * turn, 1)
                    total = piece if total is None else total + piece
                out_ref[j + i] = total.astype(dtype)
        x = lax.axis_index("dom") // (NZ * NY)
        offset = ((x + dx) % NX) * length
        mine = pltpu.roll(denom_ref[...], (cycles - offset) % cycles, 1)
        lane = lax.broadcasted_iota(jnp.int32, mine.shape, 1)
        if dtype == BF16:
            out_ref[length] = pack_denom(mine).astype(BF16)
        else:
            out_ref[length] = jnp.where(lane < length, mine, 0.0)

    return pl.pallas_call(
        kernel,
        out_shape=jax.ShapeDtypeStruct((length + 1, classes, angles), dtype),
        in_specs=[VMEM] * (ni + 2),
        out_specs=VMEM,
        compiler_params=params(24),
        cost_estimate=cost(2 * count * wide * length * angles, 0),
        name="gather_sums",
    )(resp, *images, denom)


def add_parts(own, others, ways):
    rows, classes, angles = own.shape
    length = (rows - 1) // ways

    def kernel(own_ref, *refs):
        others_ref, outs = refs[: len(others)], refs[len(others) :]
        total = own_ref[rows - 1]
        for ref in others_ref:
            total = total + ref[rows - 1].astype(F32)
        denom = join_denom(total)
        packed = pack_denom(denom).astype(BF16)
        for way in range(ways):
            for j in range(length):
                total = own_ref[way * length + j]
                for ref in others_ref:
                    total = total + ref[way * length + j].astype(F32)
                outs[way][j] = total.astype(outs[way].dtype)
            outs[way][length] = packed if way else denom

    shape = (length + 1, classes, angles)
    return pl.pallas_call(
        kernel,
        out_shape=tuple(
            jax.ShapeDtypeStruct(shape, BF16 if way else F32) for way in range(ways)
        ),
        in_specs=[VMEM] * (1 + len(others)),
        out_specs=(VMEM,) * ways,
        compiler_params=params(16),
        cost_estimate=cost(2 * 384 * 512 * 32 * 128, 0),
        name="add_parts",
    )(own, *others)


def finish(own, others):
    rows, classes, angles = own.shape

    def kernel(own_ref, *refs):
        others_ref, out_ref = refs[:-1], refs[-1]
        dom = lax.axis_index("dom")
        offset = ((dom // NY) % NZ) * (4 * NY) + (dom % NY) * 4
        denom = own_ref[rows - 1]
        for ref in others_ref:
            denom = denom + ref[rows - 1].astype(F32)
        denom = pltpu.roll(join_denom(denom), (angles - offset) % angles, 1) + TIKHONOV
        for i in range(rows - 1):
            numer = own_ref[i]
            for ref in others_ref:
                numer = numer + ref[i].astype(F32)
            out_ref[:, i, :] = numer / denom[:, i : i + 1]

    return pl.pallas_call(
        kernel,
        out_shape=jax.ShapeDtypeStruct((classes, rows - 1, angles), F32),
        in_specs=[VMEM] * (1 + len(others)),
        out_specs=VMEM,
        compiler_params=params(16),
        name="finish",
    )(own, *others)


def local(particles, references, ctf_table, noise_inv, groups, prior_rot):
    classes = references.shape[0]
    parts = 4
    particles, ctf_table, noise_inv = (
        pltpu.with_memory_space_constraint(value, pltpu.HBM)
        for value in (particles, ctf_table, noise_inv.reshape(1, -1))
    )
    from_z = send(references, 0, 1, 0)
    weight, power_pair, here = setup(groups, ctf_table, noise_inv, particles, parts)
    piece = join([references, from_z], weight, turned=True)
    from_y = [send(piece, 0, 0, -d) for d in (1, 2, 3)]
    images = []
    for part in range(parts):
        image, token, *rest = weigh(particles, here, weight, part, parts)
        here = rest[0] if rest else None
        images.append(image)
        if part == 1:
            piece = join([piece] + from_y, token)
        if part == 2:
            late = join([piece], token)
    blocks = [piece] + [send(late if d == 1 else piece, -d, 0, 0) for d in (1, 2, 3)]

    before = correlate((0,), blocks[:1], images, None)
    before = correlate((3,), [blocks[3]], images, before)
    before = correlate((2,), [blocks[2]], images, before)
    expo, stats = score((1,), [blocks[1]], images, before, power_pair, prior_rot)
    others = [lax.ppermute(stats, "cls", [(i, i ^ j) for i in range(4)]) for j in (1, 2, 3)]
    turned = turn_over(expo)
    resp, loglik, denom = share(turned, stats, others, power_pair, classes)

    arrived = []
    for d in (2, 1, 3):
        arrived.append(send(gather_sums(d, resp, images, denom, BF16), d, 0, 0))
    own = gather_sums(0, resp, images, denom, F32)
    for value in arrived[:2]:
        (own,) = add_parts(own, [value], 1)
    pieces = add_parts(own, arrived[2:], NY)
    arrived = [send(pieces[d], 0, 0, d) for d in (1, 2, 3)]
    pieces = add_parts(pieces[0], arrived, NZ)
    new_refs = finish(pieces[0], [send(pieces[1], 0, 1, 0)])
    return (new_refs, loglik[0])


def solution(mesh):
    in_specs = (P("dom", None, None), P("cls", "dom", None), P(), P(), P("dom"), P("dom"))
    out_specs = (P("cls", "dom", None), P("dom"))
    return jax.shard_map(local, mesh=mesh, in_specs=in_specs, out_specs=out_specs, check_vma=False)
```

```python
import jax
import jax.numpy as jnp
from jax import lax
from jax.experimental import pallas as pl
from jax.experimental.pallas import tpu as pltpu
from jax.sharding import PartitionSpec as P

ROTS = 16
PRIOR_WEIGHT = 0.02
TIKHONOV = 1.0
F32 = jnp.float32
BF16 = jnp.bfloat16
NX, NZ, NY = 4, 2, 4
VMEM = pl.BlockSpec(memory_space=pltpu.VMEM)
HBM = pl.BlockSpec(memory_space=pltpu.HBM)
MIB = 2**20
STREAMS = 1


def params(mib):
    return pltpu.CompilerParams(vmem_limit_bytes=mib * MIB)


def cost(flops, nbytes):
    return pl.CostEstimate(flops=flops // 64, bytes_accessed=nbytes // 64, transcendentals=0)


def coords(i):
    return i // (NZ * NY), (i // NY) % NZ, i % NY


def shift(dx, dz, dy):
    pairs = []
    for i in range(NX * NZ * NY):
        x, z, y = coords(i)
        pairs.append((i, ((x + dx) % NX) * NZ * NY + ((z + dz) % NZ) * NY + (y + dy) % NY))
    return pairs


def send(value, dx, dz, dy):
    return lax.ppermute(value, "dom", shift(dx, dz, dy))


def split2(value):
    high = value.astype(BF16)
    low = (value - high.astype(F32)).astype(BF16)
    return high, low


def load_rows(source, start, target, sems, first):
    rows = target.shape[0] // STREAMS
    return [
        pltpu.make_async_copy(
            source.at[pl.ds(start + i * rows, rows)], target.at[pl.ds(i * rows, rows)], sems.at[first + i]
        )
        for i in range(STREAMS)
    ]


def setup_kernel(groups_ref, ctf_hbm, noise_hbm, particles_hbm, weight_ref, power_ref, first_ref, ctf_ref, noise_ref, sems):
    count = groups_ref.shape[0]
    group_count, cycles = ctf_ref.shape
    copies = [
        pltpu.make_async_copy(ctf_hbm, ctf_ref, sems.at[0]),
        pltpu.make_async_copy(noise_hbm, noise_ref, sems.at[1]),
    ]
    copies += load_rows(particles_hbm, 0, first_ref, sems, 2)
    for copy in copies:
        copy.start()
    choose = (
        lax.broadcasted_iota(jnp.int32, (group_count, count), 0) == groups_ref[...].reshape(1, count)
    ).astype(F32)
    pick = lambda table: lax.dot_general(
        choose, table, (((0,), (0,)), ((), ())), precision=lax.Precision.HIGHEST,
        preferred_element_type=F32,
    )
    copies[0].wait()
    copies[1].wait()
    ctf = ctf_ref[...]
    noise = noise_ref[...]
    weight_ref[...] = pick(ctf) * noise
    high, low = split2(pick(ctf * ctf * noise))
    power_ref[:, :cycles] = high
    power_ref[:, cycles:] = low
    for copy in copies[2:]:
        copy.wait()


def setup(groups, ctf_table, noise_inv, particles, parts):
    count = groups.shape[0]
    cycles = ctf_table.shape[1]
    return pl.pallas_call(
        setup_kernel,
        out_shape=(
            jax.ShapeDtypeStruct((count, cycles), F32),
            jax.ShapeDtypeStruct((count, 2 * cycles), BF16),
            pltpu.VMEM((count // parts,) + particles.shape[1:], BF16),
        ),
        in_specs=[VMEM, HBM, HBM, HBM],
        out_specs=(VMEM, VMEM, VMEM),
        scratch_shapes=[
            pltpu.VMEM(ctf_table.shape, F32),
            pltpu.VMEM((1, cycles), F32),
            pltpu.SemaphoreType.DMA((2 + STREAMS,)),
        ],
        compiler_params=params(16),
        name="setup",
    )(groups, ctf_table, noise_inv, particles)


def weigh(particles, here, weight, part, parts):
    count, cycles, angles = particles.shape
    rows = count // parts
    pitch = cycles + 1
    last = part == parts - 1

    def kernel(particles_hbm, here_ref, weight_ref, out_ref, token_ref, *refs):
        if not last:
            next_ref, wide, sems = refs
            copies = load_rows(particles_hbm, (part + 1) * rows, next_ref, sems, 0)
            for copy in copies:
                copy.start()
        else:
            wide = refs[0]
        values = weight_ref[part * rows : (part + 1) * rows]
        token_ref[...] = values[0:8]
        for n in range(rows):
            wide[pl.ds(n * pitch, cycles), :] = here_ref[n].astype(F32)
        pair = jnp.concatenate(split2(values), axis=1)
        row = lax.broadcasted_iota(jnp.int32, (16, 2 * angles), 0)
        side = lax.broadcasted_iota(jnp.int32, (16, 2 * angles), 1) // angles
        for q in range(0, cycles, 2):
            if q % 6 < 4:
                base = q // 16 * 16
                pick = [jnp.where(row - side == q % 16, 1.0, 0.0).astype(BF16)]
                if base:
                    pick = [jnp.zeros((base, 2 * angles), BF16)] + pick
                if base + 16 < cycles:
                    pick = pick + [jnp.zeros((cycles - 16 - base, 2 * angles), BF16)]
                spread = jnp.dot(
                    pair, jnp.concatenate(pick * 2, axis=0), preferred_element_type=F32
                )
                scales = [spread[:, :angles], spread[:, angles:]]
            else:
                scales = [values[:, q : q + 1], values[:, q + 1 : q + 2]]
            for i in range(2):
                image = wide[pl.ds(q + i, rows, stride=pitch), :]
                out_ref[q + i] = (image * scales[i]).astype(BF16)
        if not last:
            for copy in copies:
                copy.wait()

    shape = (rows, cycles, angles)
    return pl.pallas_call(
        kernel,
        out_shape=(pltpu.VMEM((cycles, rows, angles), BF16), jax.ShapeDtypeStruct((8, cycles), F32))
        + (() if last else (pltpu.VMEM(shape, BF16),)),
        in_specs=[HBM, VMEM, VMEM],
        out_specs=(VMEM,) * (2 if last else 3),
        scratch_shapes=[pltpu.VMEM((rows * pitch + 8, angles), F32)]
        + ([] if last else [pltpu.SemaphoreType.DMA((STREAMS,))]),
        compiler_params=params(16),
        cost_estimate=cost(0, rows * cycles * angles * 16),
        name="weigh",
    )(particles, here, weight)


def join(pieces, *tokens, turned=False):
    rows, classes, angles = pieces[0].shape
    if turned:
        rows, classes = classes, rows

    def kernel(*refs):
        out_ref = refs[-1]
        for i, ref in enumerate(refs[: len(pieces)]):
            block = ref[...].astype(F32) if turned else None
            for j in range(rows):
                out_ref[i * rows + j] = block[:, j, :].astype(BF16) if turned else ref[j]

    return pl.pallas_call(
        kernel,
        out_shape=jax.ShapeDtypeStruct((rows * len(pieces), classes, angles), BF16),
        in_specs=[VMEM] * len(pieces) + [pl.BlockSpec(memory_space=pl.ANY)] * len(tokens),
        out_specs=VMEM,
        compiler_params=params(16),
        name="join",
    )(*pieces, *tokens)


def cycle_of(dx, j):
    dom = lax.axis_index("dom")
    x, z, y = dom // (NZ * NY), (dom // NY) % NZ, dom % NY
    dy, dz, i = j // (4 * NZ), (j // 4) % NZ, j % 4
    return ((x + dx) % NX) * (4 * NZ * NY) + ((z + dz) % NZ) * (4 * NY) + ((y + dy) % NY) * 4 + i


def correlate_steps(shifts, block_refs, image_refs, turned, total, power):
    classes, angles = block_refs[0].shape[1:]
    lane = lax.broadcasted_iota(jnp.int32, power.shape, 1)
    slot = 0
    for dx, block_ref in zip(shifts, block_refs):
        for j in range(0, block_ref.shape[0], 2):
            sides = []
            for i in range(2):
                piece = block_ref[j + i]
                cycle = cycle_of(dx, j + i)
                for turn in range(ROTS):
                    turned[slot % 4, turn * classes : (turn + 1) * classes, i * angles : (i + 1) * angles] = (
                        pltpu.roll(piece, 8 * turn, 1) if turn else piece
                    )
                wide = piece.astype(F32)
                power = jnp.where(lane == cycle, jnp.sum(wide * wide, axis=1, keepdims=True), power)
                sides.append(jnp.concatenate([ref[cycle] for ref in image_refs], axis=0))
            part = lax.dot_general(
                jnp.concatenate(sides, axis=1), turned[slot % 4], (((1,), (1,)), ((), ())),
                preferred_element_type=F32,
            )
            total = part if total is None else total + part
            slot += 1
    return total, power


def correlate(shifts, blocks, images, before):
    cycles = images[0].shape[0]
    angles = images[0].shape[2]
    count = sum(image.shape[1] for image in images)
    classes = blocks[0].shape[1]
    wide = ROTS * classes
    nb, ni = len(blocks), len(images)

    def kernel(*refs):
        block_refs, image_refs = refs[:nb], refs[nb : nb + ni]
        rest = refs[nb + ni :]
        if before is not None:
            total, power = rest[0][...], rest[1][...]
            rest = rest[2:]
        else:
            total, power = None, jnp.zeros((classes, cycles), F32)
        total_ref, power_ref, turned = rest
        total, power = correlate_steps(shifts, block_refs, image_refs, turned, total, power)
        total_ref[...] = total
        power_ref[...] = power

    extra = [] if before is None else list(before)
    return pl.pallas_call(
        kernel,
        out_shape=(pltpu.VMEM((count, wide), F32), pltpu.VMEM((classes, cycles), F32)),
        in_specs=[VMEM] * (nb + ni + len(extra)),
        out_specs=(VMEM, VMEM),
        scratch_shapes=[pltpu.VMEM((4, wide, 2 * angles), BF16)],
        compiler_params=params(24),
        cost_estimate=cost(2 * count * wide * 32 * nb * angles, 0),
        name="correlate",
    )(*blocks, *images, *extra)


def score(shifts, blocks, images, before, power_pair, prior_rot):
    cycles = images[0].shape[0]
    angles = images[0].shape[2]
    count = sum(image.shape[1] for image in images)
    classes = blocks[0].shape[1]
    wide = ROTS * classes
    nb, ni = len(blocks), len(images)

    def kernel(*refs):
        block_refs, image_refs = refs[:nb], refs[nb : nb + ni]
        total_ref, cycle_ref, pair_ref, prior_ref, expo_ref, stats_ref, turned = refs[nb + ni :]
        total, power = correlate_steps(
            shifts, block_refs, image_refs, turned, total_ref[...], cycle_ref[...]
        )
        high, low = split2(-0.5 * power)
        both = jnp.concatenate([high, high], axis=1)
        low_both = jnp.concatenate([low, low], axis=1)
        pair = pair_ref[...]
        norm = lax.dot_general(pair, both, (((1,), (1,)), ((), ())), preferred_element_type=F32)
        norm = norm + lax.dot_general(
            pair, low_both, (((1,), (1,)), ((), ())), preferred_element_type=F32
        )
        total = total + jnp.concatenate([norm] * ROTS, axis=1)
        hot = (
            lax.broadcasted_iota(jnp.int32, (2 * ROTS, count), 0) % ROTS == prior_ref[...]
        ).astype(BF16)
        row = lax.broadcasted_iota(jnp.int32, (2 * ROTS, wide), 0)
        turn = lax.broadcasted_iota(jnp.int32, (2 * ROTS, wide), 1) // classes
        offset = (turn - row + 2 * ROTS) % ROTS
        distance = jnp.minimum(offset, ROTS - offset).astype(F32)
        prior = -PRIOR_WEIGHT * distance * distance
        high, low = split2(prior)
        table = jnp.where(row < ROTS, high.astype(F32), low.astype(F32)).astype(BF16)
        total = total + lax.dot_general(
            hot, table, (((0,), (0,)), ((), ())), preferred_element_type=F32
        )
        peak = jnp.max(total, axis=1, keepdims=True)
        expo = jnp.exp(total - peak)
        expo_ref[...] = expo
        mass = jnp.sum(expo, axis=1, keepdims=True)
        lane = lax.broadcasted_iota(jnp.int32, (count, 128), 1)
        stats = jnp.transpose(jnp.where(lane < 64, peak, mass))
        stats_ref[0:8] = stats[0:8]
        stats_ref[8:16] = stats[64:72]

    return pl.pallas_call(
        kernel,
        out_shape=(pltpu.VMEM((count, wide), F32), jax.ShapeDtypeStruct((16, count), F32)),
        in_specs=[VMEM] * (nb + ni + 4),
        out_specs=(VMEM, VMEM),
        scratch_shapes=[pltpu.VMEM((4, wide, 2 * angles), BF16)],
        compiler_params=params(24),
        cost_estimate=cost(2 * count * wide * 32 * nb * angles, 0),
        name="score",
    )(*blocks, *images, *before, power_pair, prior_rot.reshape(1, count))


def turn_over_kernel(expo_ref, out_ref):
    out_ref[...] = jnp.transpose(expo_ref[...])


def turn_over(expo):
    count, wide = expo.shape
    return pl.pallas_call(
        turn_over_kernel,
        out_shape=pltpu.VMEM((wide, count), F32),
        in_specs=[VMEM],
        out_specs=VMEM,
        compiler_params=params(16),
        cost_estimate=cost(0, 4 * count * wide),
        name="turn_over",
    )(expo)


def share_kernel(expo_ref, own_ref, a_ref, b_ref, c_ref, pair_ref, resp_ref, loglik_ref, denom_ref):
    refs = (own_ref, a_ref, b_ref, c_ref)
    peaks = [ref[0:8] for ref in refs]
    peak = jnp.maximum(jnp.maximum(peaks[0], peaks[1]), jnp.maximum(peaks[2], peaks[3]))
    scales = [jnp.exp(value - peak) for value in peaks]
    total = sum(scale * ref[8:16] for scale, ref in zip(scales, refs))
    loglik_ref[...] = peak + jnp.log(total)
    factor = (scales[0] / total)[0:1]
    resp = (expo_ref[...] * factor).astype(BF16)
    resp_ref[...] = resp
    classes, cycles = denom_ref.shape
    rows = jnp.dot(resp, pair_ref[...], preferred_element_type=F32)
    rows = rows[:, :cycles] + rows[:, cycles:]
    denom = rows[:classes]
    for turn in range(1, ROTS):
        denom = denom + rows[turn * classes : (turn + 1) * classes]
    denom_ref[...] = denom


def share(expo, own, others, power_pair, classes):
    wide, count = expo.shape
    cycles = power_pair.shape[1] // 2
    return pl.pallas_call(
        share_kernel,
        out_shape=(
            pltpu.VMEM((wide, count), BF16),
            jax.ShapeDtypeStruct((8, count), F32),
            pltpu.VMEM((classes, cycles), F32),
        ),
        in_specs=[VMEM] * 6,
        out_specs=(VMEM, VMEM, VMEM),
        compiler_params=params(24),
        name="share",
    )(expo, own, *others, power_pair)


def pack_denom(denom):
    lane = lax.broadcasted_iota(jnp.int32, denom.shape, 1)
    high, low = split2(denom)
    packed = jnp.where(lane < 32, high.astype(F32), pltpu.roll(low.astype(F32), 32, 1))
    return jnp.where(lane < 64, packed, 0.0)


def join_denom(packed):
    lane = lax.broadcasted_iota(jnp.int32, packed.shape, 1)
    return jnp.where(lane < 32, packed + pltpu.roll(packed, 96, 1), 0.0)


def gather_sums(dx, resp, images, denom, dtype):
    classes, cycles = denom.shape
    angles = images[0].shape[2]
    wide, count = resp.shape
    length = 4 * NZ * NY
    ni = len(images)

    def kernel(*refs):
        resp_ref, image_refs = refs[0], refs[1 : 1 + ni]
        denom_ref, out_ref = refs[1 + ni :]
        for j in range(0, length, 2):
            side = jnp.concatenate(
                [
                    jnp.concatenate([ref[cycle_of(dx, j + i)] for ref in image_refs], axis=0)
                    for i in range(2)
                ],
                axis=1,
            )
            sums = jnp.dot(resp_ref[...], side, preferred_element_type=F32)
            for i in range(2):
                total = None
                for turn in range(ROTS):
                    piece = sums[turn * classes : (turn + 1) * classes, i * angles : (i + 1) * angles]
                    if turn:
                        piece = pltpu.roll(piece, angles - 8 * turn, 1)
                    total = piece if total is None else total + piece
                out_ref[j + i] = total.astype(dtype)
        x = lax.axis_index("dom") // (NZ * NY)
        offset = ((x + dx) % NX) * length
        mine = pltpu.roll(denom_ref[...], (cycles - offset) % cycles, 1)
        lane = lax.broadcasted_iota(jnp.int32, mine.shape, 1)
        if dtype == BF16:
            out_ref[length] = pack_denom(mine).astype(BF16)
        else:
            out_ref[length] = jnp.where(lane < length, mine, 0.0)

    return pl.pallas_call(
        kernel,
        out_shape=jax.ShapeDtypeStruct((length + 1, classes, angles), dtype),
        in_specs=[VMEM] * (ni + 2),
        out_specs=VMEM,
        compiler_params=params(24),
        cost_estimate=cost(2 * count * wide * length * angles, 0),
        name="gather_sums",
    )(resp, *images, denom)


def add_parts(own, others, ways):
    rows, classes, angles = own.shape
    length = (rows - 1) // ways

    def kernel(own_ref, *refs):
        others_ref, outs = refs[: len(others)], refs[len(others) :]
        total = own_ref[rows - 1]
        for ref in others_ref:
            total = total + ref[rows - 1].astype(F32)
        denom = join_denom(total)
        packed = pack_denom(denom).astype(BF16)
        for way in range(ways):
            for j in range(length):
                total = own_ref[way * length + j]
                for ref in others_ref:
                    total = total + ref[way * length + j].astype(F32)
                outs[way][j] = total.astype(outs[way].dtype)
            outs[way][length] = packed if way else denom

    shape = (length + 1, classes, angles)
    return pl.pallas_call(
        kernel,
        out_shape=tuple(
            jax.ShapeDtypeStruct(shape, BF16 if way else F32) for way in range(ways)
        ),
        in_specs=[VMEM] * (1 + len(others)),
        out_specs=(VMEM,) * ways,
        compiler_params=params(16),
        cost_estimate=cost(2 * 384 * 512 * 32 * 128, 0),
        name="add_parts",
    )(own, *others)


def finish(own, others):
    rows, classes, angles = own.shape

    def kernel(own_ref, *refs):
        others_ref, out_ref = refs[:-1], refs[-1]
        dom = lax.axis_index("dom")
        offset = ((dom // NY) % NZ) * (4 * NY) + (dom % NY) * 4
        denom = own_ref[rows - 1]
        for ref in others_ref:
            denom = denom + ref[rows - 1].astype(F32)
        denom = pltpu.roll(join_denom(denom), (angles - offset) % angles, 1) + TIKHONOV
        for i in range(rows - 1):
            numer = own_ref[i]
            for ref in others_ref:
                numer = numer + ref[i].astype(F32)
            out_ref[:, i, :] = numer / denom[:, i : i + 1]

    return pl.pallas_call(
        kernel,
        out_shape=jax.ShapeDtypeStruct((classes, rows - 1, angles), F32),
        in_specs=[VMEM] * (1 + len(others)),
        out_specs=VMEM,
        compiler_params=params(16),
        name="finish",
    )(own, *others)


def local(particles, references, ctf_table, noise_inv, groups, prior_rot):
    classes = references.shape[0]
    parts = 4
    particles, ctf_table, noise_inv = (
        pltpu.with_memory_space_constraint(value, pltpu.HBM)
        for value in (particles, ctf_table, noise_inv.reshape(1, -1))
    )
    from_z = send(references, 0, 1, 0)
    weight, power_pair, here = setup(groups, ctf_table, noise_inv, particles, parts)
    piece = join([references, from_z], weight, turned=True)
    from_y = [send(piece, 0, 0, -d) for d in (1, 2, 3)]
    images = []
    for part in range(parts):
        image, token, *rest = weigh(particles, here, weight, part, parts)
        here = rest[0] if rest else None
        images.append(image)
        if part == 1:
            piece = join([piece] + from_y, token)
    blocks = [piece] + [send(piece, -d, 0, 0) for d in (1, 2, 3)]

    before = correlate((0, 3), [blocks[0], blocks[3]], images, None)
    before = correlate((2,), [blocks[2]], images, before)
    expo, stats = score((1,), [blocks[1]], images, before, power_pair, prior_rot)
    others = [lax.ppermute(stats, "cls", [(i, i ^ j) for i in range(4)]) for j in (1, 2, 3)]
    turned = turn_over(expo)
    resp, loglik, denom = share(turned, stats, others, power_pair, classes)

    arrived = []
    for d in (2, 1, 3):
        arrived.append(send(gather_sums(d, resp, images, denom, BF16), d, 0, 0))
    own = gather_sums(0, resp, images, denom, F32)
    for value in arrived[:2]:
        (own,) = add_parts(own, [value], 1)
    pieces = add_parts(own, arrived[2:], NY)
    arrived = [send(pieces[d], 0, 0, d) for d in (1, 2, 3)]
    pieces = add_parts(pieces[0], arrived, NZ)
    new_refs = finish(pieces[0], [send(pieces[1], 0, 1, 0)])
    return (new_refs, loglik[0])


def solution(mesh):
    in_specs = (P("dom", None, None), P("cls", "dom", None), P(), P(), P("dom"), P("dom"))
    out_specs = (P("cls", "dom", None), P("dom"))
    return jax.shard_map(local, mesh=mesh, in_specs=in_specs, out_specs=out_specs, check_vma=False)
```
